32 devices in a mesh: ch: 2 (over core), ty: 4 (over z), tx: 4 (over y, x).
Axes of the slice: x: 2, y: 2, z: 4, core: 2. Of those that a mesh axis runs over, the one named last changes fastest.
Arguments:
- image_plane: bfloat16 [4, 1024, 8192], P('ch', 'ty', 'tx'), may hold values from -12 to 12
- patch_shift: int32 [4, 2, 16, 128], P('ch', None, 'ty', 'tx'), may hold values from -36 to 36, as said below
Outputs:
- corrected: bfloat16 [4, 1024, 8192], P('ch', 'ty', 'tx')
The draws below stay inside these ranges and needn't reach their ends.
Inputs may be any that keep to these rules, and one draw needn't show every extreme that they name: `patch_shift`: row components (index 0 of the second dimension) lie within -10 to 10 and reach both ends; column components reach both ends of the range.
All inputs are finite; a program needn't handle non-finite values.
Results may differ from the reference program's by a relative error of at most 0.034.
Values may be sent and summed in bfloat16 or wider, within the bound.
A program may use at most 64 MiB of HBM per device.

```python
import math
import jax
import jax.numpy as jnp
from jax import lax

CHANNELS = 4
R_DEV = 256
C_DEV = 2048
PATCH = 64
SPAN_Y = 256
SPAN_X = 512
MAX_Y = 12
MAX_X = 60
HALO_Y = 16
HALO_X = 64
NROWS = 1024
NCOLS = 8192
NPY = 16
NPX = 128
KY = 7
KX = 19
N_TY = 4


def draw_image_plane(key, part):
    key_scale, key_row, key_col, key_noise = jax.random.split(jax.random.fold_in(key, 11), 4)
    low_factor = 0.4
    scales = jnp.exp(jax.random.uniform(key_scale, (CHANNELS, NROWS // PATCH, NCOLS // PATCH), jnp.float32, math.log(0.3), math.log(3.0)))
    full_scale = jnp.repeat(jnp.repeat(scales, PATCH, axis=1), PATCH, axis=2)
    row_factor = jnp.exp(jax.random.uniform(key_row, (CHANNELS, NROWS, 1), jnp.float32, math.log(low_factor), 0.0))
    col_factor = jnp.exp(jax.random.uniform(key_col, (CHANNELS, 1, NCOLS), jnp.float32, math.log(low_factor), 0.0))
    noise_vals = jnp.clip(jax.random.normal(key_noise, (CHANNELS, NROWS, NCOLS), jnp.float32), -4.0, 4.0)
    return (noise_vals * full_scale * row_factor * col_factor).astype(jnp.bfloat16)


def draw_patch_shift(key, part):
    keys_all = jax.random.split(jax.random.fold_in(key, 23), 6)
    rows_per = R_DEV // PATCH
    cols_per = C_DEV // PATCH
    band_rows = NPY // rows_per
    band_cols = NPX // cols_per
    base_rows = jax.random.randint(keys_all[0], (CHANNELS, 1, 1), -4, 5)
    base_cols = jax.random.randint(keys_all[1], (CHANNELS, 1, 1), -15, 16)
    off_rows = jax.random.randint(keys_all[2], (CHANNELS, band_rows, band_cols), -5, 6)
    off_cols = jax.random.randint(keys_all[3], (CHANNELS, band_rows, band_cols), -20, 21)
    off_rows = jnp.repeat(jnp.repeat(off_rows, rows_per, axis=1), cols_per, axis=2)
    off_cols = jnp.repeat(jnp.repeat(off_cols, rows_per, axis=1), cols_per, axis=2)
    noise_rows = jax.random.randint(keys_all[4], (CHANNELS, NPY, NPX), -2, 3)
    noise_cols = jax.random.randint(keys_all[5], (CHANNELS, NPY, NPX), -2, 3)
    row_part = jnp.clip(base_rows + off_rows + noise_rows, -10, 10)
    col_part = jnp.clip(base_cols + off_cols + noise_cols, -36, 36)
    result = jnp.stack([row_part, col_part], axis=1).astype(jnp.int32)
    result = result.at[0, 0, 0, 0].set(10).at[0, 0, NPY - 1, NPX - 1].set(-10)
    result = result.at[0, 1, 0, 0].set(36).at[0, 1, NPY - 1, NPX - 1].set(-36)
    return result


def setup_inputs(seed: int = 0) -> dict:
    key_list = jax.random.split(jax.random.key(seed), 3)
    image_plane = draw_image_plane(jax.random.fold_in(key_list[2], 71), 0)
    patch_shift = draw_patch_shift(jax.random.fold_in(key_list[2], 71), 0)
    return dict(image_plane=image_plane, patch_shift=patch_shift)


EPS = 1e-05

def bspline(offset):
    mag = jnp.abs(offset)
    near_part = 2.0 / 3.0 - mag * mag + 0.5 * mag * mag * mag
    far_part = (2.0 - mag) * (2.0 - mag) * (2.0 - mag) / 6.0
    return jnp.where(mag < 1.0, near_part, jnp.where(mag < 2.0, far_part, 0.0 * mag))

def cubic_kernel(offset):
    mag = jnp.abs(offset)
    near_part = (1.5 * mag - 2.5) * mag * mag + 1.0
    far_part = ((-0.5 * mag + 2.5) * mag - 4.0) * mag + 2.0
    return jnp.where(mag <= 1.0, near_part, jnp.where(mag < 2.0, far_part, 0.0 * mag))

def spline_basis(centers, control_count, spacing):
    knot_pos = jnp.arange(control_count, dtype=jnp.float32) - 1.0
    return bspline(centers[:, None] / spacing - knot_pos[None, :])

def penalty(control_count):
    identity = jnp.eye(control_count, dtype=jnp.float32)
    second_diff = identity[:-2] - 2.0 * identity[1:-1] + identity[2:]
    return jnp.dot(second_diff.T, second_diff, precision=lax.Precision.HIGHEST)

def reference(image_plane, patch_shift):
    highest = lax.Precision.HIGHEST

    def plane_energy(one_plane):
        squared = one_plane.astype(jnp.float32) * one_plane.astype(jnp.float32)
        return squared.reshape(NPY, PATCH, NPX, PATCH).mean(axis=(1, 3)) + EPS
    energy = lax.map(plane_energy, image_plane)
    weight = jnp.sqrt(energy[0][None] * energy)
    shifts = patch_shift.astype(jnp.float32)
    patch_rows = jnp.arange(NPY, dtype=jnp.float32) * PATCH + PATCH / 2.0
    patch_cols = jnp.arange(NPX, dtype=jnp.float32) * PATCH + PATCH / 2.0
    row_basis = spline_basis(patch_rows, KY, SPAN_Y)
    col_basis = spline_basis(patch_cols, KX, SPAN_X)
    row_gram = jnp.einsum('ik,ci,il->ckl', row_basis, weight.sum(axis=2), row_basis, precision=highest)
    row_rhs = jnp.einsum('ik,ci->ck', row_basis, (weight * shifts[:, 0]).sum(axis=2), precision=highest)
    col_gram = jnp.einsum('jk,cj,jl->ckl', col_basis, weight.sum(axis=1), col_basis, precision=highest)
    col_rhs = jnp.einsum('jk,cj->ck', col_basis, (weight * shifts[:, 1]).sum(axis=1), precision=highest)
    lam_rows = SPAN_Y / PATCH * (NCOLS / PATCH) * (2.0 * R_DEV / SPAN_Y) ** 4
    lam_cols = SPAN_X / PATCH * (NROWS / PATCH) * (1.0 * C_DEV / SPAN_X) ** 4
    row_coef = jnp.linalg.solve(row_gram + lam_rows * penalty(KY), row_rhs[..., None])[..., 0]
    col_coef = jnp.linalg.solve(col_gram + lam_cols * penalty(KX), col_rhs[..., None])[..., 0]
    pixel_rows = jnp.arange(NROWS, dtype=jnp.float32) + 0.5
    pixel_cols = jnp.arange(NCOLS, dtype=jnp.float32) + 0.5
    row_disp = MAX_Y * jnp.tanh(jnp.einsum('yk,ck->cy', spline_basis(pixel_rows, KY, SPAN_Y), row_coef, precision=highest) / MAX_Y)
    col_disp = MAX_X * jnp.tanh(jnp.einsum('xk,ck->cx', spline_basis(pixel_cols, KX, SPAN_X), col_coef, precision=highest) / MAX_X)
    padded = jnp.pad(image_plane, ((0, 0), (HALO_Y, HALO_Y), (HALO_X, HALO_X)))
    block_cols = min(512, C_DEV)
    block_count = NCOLS // block_cols
    source_rows = jnp.arange(R_DEV + 2 * HALO_Y, dtype=jnp.float32)
    out_rows = jnp.arange(R_DEV, dtype=jnp.float32)
    source_cols = jnp.arange(block_cols + 2 * HALO_X, dtype=jnp.float32)
    out_cols = jnp.arange(block_cols, dtype=jnp.float32)

    def one_block(item_index):
        chan = item_index // N_TY
        band = item_index % N_TY
        source = lax.dynamic_slice(padded, (chan, band * R_DEV, jnp.int32(0)), (1, R_DEV + 2 * HALO_Y, NCOLS + 2 * HALO_X))[0]
        band_disp = lax.dynamic_slice(row_disp, (chan, band * R_DEV), (1, R_DEV))[0]
        row_taps = cubic_kernel(source_rows[:, None] - (out_rows[None, :] + HALO_Y + band_disp[None, :])).astype(jnp.bfloat16)
        rows_done = jnp.dot(row_taps.T.astype(jnp.float32), source.astype(jnp.float32), preferred_element_type=jnp.float32).astype(jnp.bfloat16)
        chan_disp = lax.dynamic_index_in_dim(col_disp, chan, 0, keepdims=False)

        def one_cols(block_index):
            start = block_index * block_cols
            window = lax.dynamic_slice_in_dim(rows_done, start, block_cols + 2 * HALO_X, axis=1)
            block_disp = lax.dynamic_slice_in_dim(chan_disp, start, block_cols, axis=0)
            col_taps = cubic_kernel(source_cols[:, None] - (out_cols[None, :] + HALO_X + block_disp[None, :])).astype(jnp.bfloat16)
            return jnp.dot(window.astype(jnp.float32), col_taps.astype(jnp.float32), preferred_element_type=jnp.float32).astype(jnp.bfloat16)
        pieces = lax.map(one_cols, jnp.arange(block_count, dtype=jnp.int32))
        return jnp.transpose(pieces, (1, 0, 2)).reshape(R_DEV, NCOLS)
    blocks = lax.map(one_block, jnp.arange(CHANNELS * N_TY, dtype=jnp.int32))
    return blocks.reshape(CHANNELS, NROWS, NCOLS)
```

```python
import functools

import jax
import jax.numpy as jnp
from jax import lax
from jax.experimental import pallas as pl
from jax.experimental.pallas import tpu as pltpu
from jax.sharding import PartitionSpec as P

PATCH = 64
SPAN_Y = 256
SPAN_X = 512
MAX_Y = 12
MAX_X = 60
HY = 16
HX = 128
EPS = 1e-05
LANES = 128
MESH = pl.DeviceIdType.MESH


def bspline(offset):
    mag = jnp.abs(offset)
    near_part = 2.0 / 3.0 - mag * mag + 0.5 * mag * mag * mag
    far_part = (2.0 - mag) * (2.0 - mag) * (2.0 - mag) / 6.0
    return jnp.where(mag < 1.0, near_part, jnp.where(mag < 2.0, far_part, 0.0))


def cubic_kernel(offset):
    a = jnp.maximum(2.0 - jnp.abs(offset), 0.0)
    c = a - 1.0
    b = jnp.maximum(c, 0.0)
    return a * a * (0.5 * c) + b * b * (1.0 - 2.0 * b)


def penalty_band(count):
    band = [[0.0] * count for _ in range(4)]
    coef = (1.0, -2.0, 1.0)
    for q in range(count - 2):
        for a in range(3):
            for b in range(a, 3):
                band[b - a][q + a] += coef[a] * coef[b]
    return band


def iota(dim, shape=(8, LANES)):
    return lax.broadcasted_iota(jnp.int32, shape, dim)


def repeat_for(start, stop, body):
    if stop - start <= 16:
        for i in range(start, stop):
            body(i)
    else:
        lax.fori_loop(start, stop, lambda i, _: (body(i), 0)[1], 0)


def fit_kernel(n_ty, n_tx, lam_y, lam_x, img_hbm, shift_ref, pad_hbm, col_ref, row_ref,
               img_v, sums_v, shift_v, e0_v, msg_v, slots_v, coef_v, zero_r, zero_c,
               img_sem, own_sem, zero_sem, e0_send, e0_recv, msg_send, msg_recv,
               halo_send, halo_recv):
    chans, rows, cols = img_v.shape
    prow, pcol = rows // PATCH, cols // PATCH
    n = n_ty * n_tx
    ch, ty, tx = lax.axis_index("ch"), lax.axis_index("ty"), lax.axis_index("tx")
    me = ty * n_tx + tx

    def peer_id(p):
        peer = lax.rem(me + p, n)
        return peer, {"ty": peer // n_tx, "tx": lax.rem(peer, n_tx)}

    barrier = pltpu.get_barrier_semaphore()
    partner = {"ch": 1 - ch}
    pl.semaphore_signal(barrier, inc=1, device_id=partner, device_id_type=MESH)

    def greet(p):
        _, where = peer_id(p)
        pl.semaphore_signal(barrier, inc=1, device_id=where, device_id_type=MESH)

    loads = []
    for c in range(chans):
        for i in range(prow):
            copy = pltpu.make_async_copy(
                img_hbm.at[c, pl.ds(i * PATCH, PATCH)],
                img_v.at[c, pl.ds(i * PATCH, PATCH)],
                img_sem.at[c * prow + i],
            )
            copy.start()
            loads.append(copy)
    repeat_for(1, n, greet)
    zero_r[...] = jnp.zeros_like(zero_r)
    zero_c[...] = jnp.zeros_like(zero_c)

    sub, lane = iota(0), iota(1)
    per_chan = 2 * prow
    per_dev = chans * per_chan
    ty_block = LANES // per_dev
    blocks = (n_ty + ty_block - 1) // ty_block
    col_sys = sub < chans
    row_sys = (sub >= chans) & (sub < 2 * chans)
    is_rhs = jnp.where(col_sys, (lane // pcol) % 2, (lane // prow) % 2) == 1
    key_y = n_ty * rows // SPAN_Y + 3
    key_x = n_tx * cols // SPAN_X + 3
    per_y, per_x = rows * ty_block // SPAN_Y, cols // SPAN_X
    keys = max(key_y, key_x)
    chunks = max(n_tx, blocks)
    col_pos = (lane % pcol * PATCH).astype(jnp.float32) / SPAN_X + (PATCH / 2.0 / SPAN_X + 1.0)
    row_index = lane // per_dev * prow + lane % prow
    row_pos = (row_index * PATCH).astype(jnp.float32) / SPAN_Y + (PATCH / 2.0 / SPAN_Y + 1.0)
    for q in range(2):
        for c in range(chans):
            part = shift_ref[c, q].astype(jnp.float32)
            for g in range(LANES // pcol):
                shift_v[q, pl.ds(c * prow, prow), pl.ds(g * pcol, pcol)] = part
    ind = (iota(0, (LANES, LANES)) // PATCH == iota(1, (LANES, LANES)) % 2).astype(jnp.float32)

    for c in range(chans):
        for i in range(prow):
            loads[c * prow + i].wait()
            for t in range(cols // LANES):
                part = img_v[c, pl.ds(i * PATCH, PATCH), pl.ds(t * LANES, LANES)].astype(jnp.float32)
                sums_v[pl.ds(t * 8 + c * prow + i, 1), :] = jnp.sum(part * part, axis=0, keepdims=True)
    owns = [
        pltpu.make_async_copy(
            img_v.at[c], pad_hbm.at[c, pl.ds(HY, rows), pl.ds(HX, cols)], own_sem.at[c]
        )
        for c in range(chans)
    ]
    halves = jnp.dot(sums_v[...], ind, precision=lax.Precision.HIGHEST,
                     preferred_element_type=jnp.float32)
    energy = jnp.zeros((8, LANES), jnp.float32)
    for t in range(cols // LANES):
        energy = jnp.where(lane % pcol // 2 == t, halves[t * 8 : t * 8 + 8], energy)
    energy = energy / (PATCH * PATCH) + EPS

    pl.semaphore_wait(barrier, n)
    e0_copy = pltpu.make_async_remote_copy(
        src_ref=e0_v, dst_ref=e0_v, send_sem=e0_send, recv_sem=e0_recv,
        device_id=partner, device_id_type=MESH,
    )

    @pl.when(ch == 0)
    def _():
        e0_v[...] = energy
        e0_copy.start()

    @pl.when(ch == 1)
    def _():
        e0_copy.wait_recv()

    ref_energy = jnp.concatenate([e0_v[0:prow]] * chans, axis=0)
    weight = jnp.sqrt(ref_energy * energy)
    mine = sub // prow == lane // (2 * pcol)
    scaled = jnp.where((lane // pcol) % 2 == 1, weight * shift_v[1], weight)
    msg_v[0:1, :] = jnp.sum(jnp.where(mine, scaled, 0.0), axis=0, keepdims=True)
    first = lane < pcol
    w_rows = jnp.sum(jnp.where(first, weight, 0.0), axis=1, keepdims=True)
    ws_rows = jnp.sum(jnp.where(first, weight * shift_v[0], 0.0), axis=1, keepdims=True)
    base = lax.rem(ty, ty_block) * per_dev + sub // prow * per_chan + sub % prow
    spread = jnp.where(lane == base, w_rows, jnp.where(lane == base + prow, ws_rows, 0.0))
    msg_v[1:2, :] = jnp.sum(spread, axis=0, keepdims=True)
    slots_v[me, 0:2] = msg_v[0:2]

    def msg_copy(p, slot):
        _, where = peer_id(p)
        return pltpu.make_async_remote_copy(
            src_ref=msg_v.at[pl.ds(0, 2)], dst_ref=slots_v.at[slot, pl.ds(0, 2)],
            send_sem=msg_send.at[p], recv_sem=msg_recv.at[slot],
            device_id=where, device_id_type=MESH,
        )

    repeat_for(1, n, lambda p: msg_copy(p, me).start())

    span_y = {1: (rows - HY, 0, HY), -1: (0, HY + rows, HY), 0: (0, HY, rows)}
    span_x = {1: (cols - HX, 0, HX), -1: (0, HX + cols, HX), 0: (0, HX, cols)}
    sides = [(0, 1), (0, -1), (1, 0), (-1, 0), (1, 1), (1, -1), (-1, 1), (-1, -1)]
    halos, fills = [], []
    for s, (dy, dx) in enumerate(sides):
        sy, qy, ly = span_y[dy]
        sx, qx, lx = span_x[dx]
        dst = pad_hbm.at[:, pl.ds(qy, ly), pl.ds(qx, lx)]
        to_y, to_x = ty + dy, tx + dx
        from_y, from_x = ty - dy, tx - dx
        has_to = (to_y >= 0) & (to_y < n_ty) & (to_x >= 0) & (to_x < n_tx)
        has_from = (from_y >= 0) & (from_y < n_ty) & (from_x >= 0) & (from_x < n_tx)
        halo = pltpu.make_async_remote_copy(
            src_ref=img_v.at[:, pl.ds(sy, ly), pl.ds(sx, lx)], dst_ref=dst,
            send_sem=halo_send.at[s], recv_sem=halo_recv.at[s],
            device_id={"ty": to_y, "tx": to_x}, device_id_type=MESH,
        )
        zeros = zero_c if ly == rows else zero_r
        fill = pltpu.make_async_copy(
            zeros.at[:, pl.ds(0, ly), pl.ds(0, lx)], dst, zero_sem.at[s]
        )
        pl.when(has_to)(halo.start)
        pl.when(jnp.logical_not(has_from))(fill.start)
        halos.append((halo, has_to, has_from, fill))
    for own in owns:
        own.start()

    bases = {}
    for t in range(chunks):
        span = set()
        if t < n_tx:
            span |= set(range(t * per_x, t * per_x + per_x + 3))
        if t < blocks:
            span |= set(range(t * per_y, t * per_y + per_y + 3))
        for k in sorted(span):
            if k < keys:
                local = jnp.where(col_sys, col_pos + (t * per_x - k), row_pos + (t * per_y - k))
                bases[k, t] = bspline(local.astype(jnp.float32))

    def msg_wait(p):
        peer, _ = peer_id(p)
        msg_copy(p, peer).wait_recv()

    repeat_for(1, n, msg_wait)

    data_w, data_r = [], []
    for t in range(chunks):
        data = jnp.zeros((8, LANES), jnp.float32)
        if t < n_tx:
            total = slots_v[t, 0:1]
            for y in range(1, n_ty):
                total = total + slots_v[y * n_tx + t, 0:1]
            data = jnp.where(col_sys & (lane // (2 * pcol) == sub), total, data)
        if t < blocks:
            low, high = t * ty_block * n_tx, min(n_ty, (t + 1) * ty_block) * n_tx
            total = slots_v[low, 1:2]
            for y in range(low + 1, high):
                total = total + slots_v[y, 1:2]
            data = jnp.where(row_sys & (lane % per_dev // per_chan == sub - chans), total, data)
        data_w.append(jnp.where(is_rhs, 0.0, data))
        data_r.append(jnp.where(is_rhs, data, 0.0))

    pen_y, pen_x = penalty_band(key_y), penalty_band(key_x)

    def added(d, k):
        rest = 1.0 if d == 0 else 0.0
        at_x = lam_x * pen_x[d][k] if k < key_x else rest
        at_y = lam_y * pen_y[d][k] if k < key_y else rest
        if at_x == at_y == rest:
            return rest
        return jnp.where(col_sys, at_x, jnp.where(row_sys, at_y, rest))

    band, rhs = {}, []
    for k in range(keys):
        for d in range(4):
            if k + d >= keys:
                continue
            total = None
            for t in range(chunks):
                if (k, t) in bases and (k + d, t) in bases:
                    term = bases[k, t] * bases[k + d, t] * data_w[t]
                    total = term if total is None else total + term
            if total is None:
                band[k, d] = jnp.zeros((8, LANES), jnp.float32) + added(d, k)
            else:
                band[k, d] = jnp.broadcast_to(jnp.sum(total, axis=1, keepdims=True), (8, LANES)) + added(d, k)
        total = None
        for t in range(chunks):
            if (k, t) in bases:
                term = bases[k, t] * data_r[t]
                total = term if total is None else total + term
        rhs.append(jnp.broadcast_to(jnp.sum(total, axis=1, keepdims=True), (8, LANES)))

    recips = []
    for k in range(keys):
        recip = 1.0 / band[k, 0]
        recips.append(recip)
        for e in range(1, 4):
            if k + e >= keys:
                break
            factor = band[k, e] * recip
            for f in range(e, 4):
                if k + f < keys:
                    band[k + e, f - e] = band[k + e, f - e] - factor * band[k, f]
            rhs[k + e] = rhs[k + e] - factor * rhs[k]
    solved = [None] * keys
    for k in reversed(range(keys)):
        value = rhs[k]
        for e in range(3, 0, -1):
            if k + e < keys:
                value = value - band[k, e] * solved[k + e]
        solved[k] = value * recips[k]
        coef_v[k] = solved[k]

    lane_f = lane.astype(jnp.float32) + 0.5
    for out_ref, span, size, start, bound in (
        (col_ref, SPAN_X, cols, tx * (cols // SPAN_X), MAX_X),
        (row_ref, SPAN_Y, rows, ty * (rows // SPAN_Y), MAX_Y),
    ):
        tiles = span // LANES
        shape = [
            [bspline((lane_f + u * LANES) / span - e + 1.0) for e in range(4)] for u in range(tiles)
        ]
        for q in range(size // span):
            coefs = [coef_v[start + q + e] for e in range(4)]
            for u in range(tiles):
                total = coefs[0] * shape[u][0]
                for e in range(1, 4):
                    total = total + coefs[e] * shape[u][e]
                at = (q * tiles + u) * LANES
                out_ref[:, at : at + LANES] = bound * jnp.tanh(total / bound)

    for halo, has_to, has_from, fill in halos:
        pl.when(has_from)(halo.wait_recv)
        pl.when(jnp.logical_not(has_from))(fill.wait)
        pl.when(has_to)(halo.wait_send)
    for own in owns:
        own.wait()
    pl.when(ch == 0)(e0_copy.wait_send)
    repeat_for(1, n, lambda p: msg_copy(p, me).wait_send())


BLOCK = 256
HALF = 128


def warp_kernel(pad_ref, col_ref, row_ref, out_ref, rows_v, rtaps_v, ctaps_v):
    c, b = pl.program_id(0), pl.program_id(1)
    rows = out_ref.shape[1]
    depth = pad_ref.shape[1]

    @pl.when((c == 0) & (b == 0))
    def _():
        ctaps_v[...] = jnp.zeros_like(ctaps_v)

    @pl.when(b == 0)
    def _():
        rows_v[...] = jnp.zeros_like(rows_v)
        disp = jnp.where(c == 0, row_ref[2:3, :], row_ref[3:4, :])
        target = lax.broadcasted_iota(jnp.int32, (1, rows), 1).astype(jnp.float32) + HY + disp
        source = lax.broadcasted_iota(jnp.int32, (depth, rows), 0).astype(jnp.float32)
        rtaps_v[...] = cubic_kernel(source - target).T.astype(jnp.bfloat16)

    rows_v[:, 0:BLOCK] = rows_v[:, BLOCK : 2 * BLOCK]
    rows_v[:, BLOCK : 2 * BLOCK] = jnp.dot(
        rtaps_v[...], pad_ref[0], preferred_element_type=jnp.float32
    ).astype(jnp.bfloat16)
    first = jnp.maximum(b - 1, 0) * BLOCK
    source = lax.broadcasted_iota(jnp.int32, (2 * HALF, HALF), 0).astype(jnp.float32)
    for h in range(BLOCK // HALF):
        at = pl.ds(pl.multiple_of(first + h * HALF, HALF), HALF)
        disp = jnp.where(c == 0, col_ref[0:1, at], col_ref[1:2, at])
        target = lax.broadcasted_iota(jnp.int32, (1, HALF), 1).astype(jnp.float32) + 64.0 + disp
        ctaps_v[64 + h * HALF : 64 + h * HALF + 2 * HALF, h * HALF : (h + 1) * HALF] = cubic_kernel(
            source - target
        ).astype(jnp.bfloat16)
    out_ref[0] = jnp.dot(
        rows_v[...], ctaps_v[...], preferred_element_type=jnp.float32
    ).astype(jnp.bfloat16)


def local(image_plane, patch_shift):
    n_ty, n_tx = lax.axis_size("ty"), lax.axis_size("tx")
    chans, rows, cols = image_plane.shape
    n = n_ty * n_tx
    lam_y = SPAN_Y / PATCH * (cols * n_tx / PATCH) * (2.0 * rows / SPAN_Y) ** 4
    lam_x = SPAN_X / PATCH * (rows * n_ty / PATCH) * (1.0 * cols / SPAN_X) ** 4
    keys = max(n_ty * rows // SPAN_Y, n_tx * cols // SPAN_X) + 3
    high, wide = rows + 2 * HY, cols + 2 * HX
    f32 = jnp.float32
    dma = pltpu.SemaphoreType.DMA
    vmem = pl.BlockSpec(memory_space=pltpu.VMEM)
    hbm = pl.BlockSpec(memory_space=pl.ANY)
    padded, col_disp, row_disp = pl.pallas_call(
        functools.partial(fit_kernel, n_ty, n_tx, lam_y, lam_x),
        out_shape=(
            jax.ShapeDtypeStruct((chans, high, wide), jnp.bfloat16),
            jax.ShapeDtypeStruct((8, cols), f32),
            jax.ShapeDtypeStruct((8, rows), f32),
        ),
        in_specs=[hbm, vmem],
        out_specs=(hbm, vmem, vmem),
        scratch_shapes=[
            pltpu.VMEM((chans, rows, cols), jnp.bfloat16),
            pltpu.VMEM((LANES, LANES), f32),
            pltpu.VMEM((2, 8, LANES), f32),
            pltpu.VMEM((8, LANES), f32),
            pltpu.VMEM((8, LANES), f32),
            pltpu.VMEM((n, 8, LANES), f32),
            pltpu.VMEM((keys, 8, LANES), f32),
            pltpu.VMEM((chans, HY, cols), jnp.bfloat16),
            pltpu.VMEM((chans, rows, HX), jnp.bfloat16),
            dma((8,)), dma((chans,)), dma((8,)), dma, dma,
            dma((n,)), dma((n,)), dma((8,)), dma((8,)),
        ],
        compiler_params=pltpu.CompilerParams(
            collective_id=0, has_side_effects=True, vmem_limit_bytes=32 * 2**20
        ),
    )(image_plane, patch_shift)
    steps = cols // BLOCK
    return pl.pallas_call(
        warp_kernel,
        grid=(chans, steps + 1),
        out_shape=jax.ShapeDtypeStruct((chans, rows, cols), jnp.bfloat16),
        in_specs=[
            pl.BlockSpec((1, high, BLOCK), lambda c, b: (c, 0, b)),
            pl.BlockSpec((8, cols), lambda c, b: (0, 0)),
            pl.BlockSpec((8, rows), lambda c, b: (0, 0)),
        ],
        out_specs=pl.BlockSpec((1, rows, BLOCK), lambda c, b: (c, 0, jnp.maximum(b - 1, 0))),
        scratch_shapes=[
            pltpu.VMEM((rows, 2 * BLOCK), jnp.bfloat16),
            pltpu.VMEM((rows, high), jnp.bfloat16),
            pltpu.VMEM((2 * BLOCK, BLOCK), jnp.bfloat16),
        ],
        compiler_params=pltpu.CompilerParams(vmem_limit_bytes=32 * 2**20),
    )(padded, col_disp, row_disp)


def solution(mesh):
    return jax.shard_map(
        local,
        mesh=mesh,
        in_specs=(P("ch", "ty", "tx"), P("ch", None, "ty", "tx")),
        out_specs=P("ch", "ty", "tx"),
        check_vma=False,
    )
```

```python
import functools

import jax
import jax.numpy as jnp
from jax import lax
from jax.experimental import pallas as pl
from jax.experimental.pallas import tpu as pltpu
from jax.sharding import PartitionSpec as P

PATCH = 64
SPAN_Y = 256
SPAN_X = 512
MAX_Y = 12
MAX_X = 60
HY = 16
HX = 128
EPS = 1e-05
LANES = 128
MESH = pl.DeviceIdType.MESH


def bspline(offset):
    mag = jnp.abs(offset)
    near_part = 2.0 / 3.0 - mag * mag + 0.5 * mag * mag * mag
    far_part = (2.0 - mag) * (2.0 - mag) * (2.0 - mag) / 6.0
    return jnp.where(mag < 1.0, near_part, jnp.where(mag < 2.0, far_part, 0.0))


def cubic_kernel(offset):
    a = jnp.maximum(2.0 - jnp.abs(offset), 0.0)
    c = a - 1.0
    b = jnp.maximum(c, 0.0)
    return a * a * (0.5 * c) + b * b * (1.0 - 2.0 * b)


def penalty_band(count):
    band = [[0.0] * count for _ in range(4)]
    coef = (1.0, -2.0, 1.0)
    for q in range(count - 2):
        for a in range(3):
            for b in range(a, 3):
                band[b - a][q + a] += coef[a] * coef[b]
    return band


def iota(dim, shape=(8, LANES)):
    return lax.broadcasted_iota(jnp.int32, shape, dim)


def repeat_for(start, stop, body):
    if stop - start <= 16:
        for i in range(start, stop):
            body(i)
    else:
        lax.fori_loop(start, stop, lambda i, _: (body(i), 0)[1], 0)


def fit_kernel(n_ty, n_tx, lam_y, lam_x, img_hbm, shift_hbm, pad_hbm, col_ref, row_ref,
               img_v, shift_ref, sums_v, shift_v, e0_v, msg_v, slots_v, coef_v, zero_r, zero_c,
               img_sem, shift_sem, own_sem, zero_sem, e0_send, e0_recv, msg_send, msg_recv,
               halo_send, halo_recv):
    chans, rows, cols = img_v.shape
    prow, pcol = rows // PATCH, cols // PATCH
    n = n_ty * n_tx
    ch, ty, tx = lax.axis_index("ch"), lax.axis_index("ty"), lax.axis_index("tx")
    me = ty * n_tx + tx

    def peer_id(p):
        peer = lax.rem(me + p, n)
        return peer, {"ty": peer // n_tx, "tx": lax.rem(peer, n_tx)}

    barrier = pltpu.get_barrier_semaphore()
    partner = {"ch": 1 - ch}
    pl.semaphore_signal(barrier, inc=1, device_id=partner, device_id_type=MESH)

    def greet(p):
        _, where = peer_id(p)
        pl.semaphore_signal(barrier, inc=1, device_id=where, device_id_type=MESH)

    shift_load = pltpu.make_async_copy(shift_hbm, shift_ref, shift_sem)
    shift_load.start()
    loads = []
    for c in range(chans):
        for i in range(prow):
            copy = pltpu.make_async_copy(
                img_hbm.at[c, pl.ds(i * PATCH, PATCH)],
                img_v.at[c, pl.ds(i * PATCH, PATCH)],
                img_sem.at[c * prow + i],
            )
            copy.start()
            loads.append(copy)
    repeat_for(1, n, greet)
    zero_r[...] = jnp.zeros_like(zero_r)
    zero_c[...] = jnp.zeros_like(zero_c)

    sub, lane = iota(0), iota(1)
    per_chan = 2 * prow
    per_dev = chans * per_chan
    ty_block = LANES // per_dev
    blocks = (n_ty + ty_block - 1) // ty_block
    col_sys = sub < chans
    row_sys = (sub >= chans) & (sub < 2 * chans)
    is_rhs = jnp.where(col_sys, (lane // pcol) % 2, (lane // prow) % 2) == 1
    key_y = n_ty * rows // SPAN_Y + 3
    key_x = n_tx * cols // SPAN_X + 3
    per_y, per_x = rows * ty_block // SPAN_Y, cols // SPAN_X
    keys = max(key_y, key_x)
    chunks = max(n_tx, blocks)
    col_pos = (lane % pcol * PATCH).astype(jnp.float32) / SPAN_X + (PATCH / 2.0 / SPAN_X + 1.0)
    row_index = lane // per_dev * prow + lane % prow
    row_pos = (row_index * PATCH).astype(jnp.float32) / SPAN_Y + (PATCH / 2.0 / SPAN_Y + 1.0)
    shift_load.wait()
    for q in range(2):
        for c in range(chans):
            part = shift_ref[c, q].astype(jnp.float32)
            for g in range(LANES // pcol):
                shift_v[q, pl.ds(c * prow, prow), pl.ds(g * pcol, pcol)] = part
    ind = (iota(0, (LANES, LANES)) // PATCH == iota(1, (LANES, LANES)) % 2).astype(jnp.float32)

    for c in range(chans):
        for i in range(prow):
            loads[c * prow + i].wait()
            for t in range(cols // LANES):
                part = img_v[c, pl.ds(i * PATCH, PATCH), pl.ds(t * LANES, LANES)].astype(jnp.float32)
                sums_v[pl.ds(t * 8 + c * prow + i, 1), :] = jnp.sum(part * part, axis=0, keepdims=True)
    owns = [
        pltpu.make_async_copy(
            img_v.at[c], pad_hbm.at[c, pl.ds(HY, rows), pl.ds(HX, cols)], own_sem.at[c]
        )
        for c in range(chans)
    ]
    halves = jnp.dot(sums_v[...], ind, precision=lax.Precision.HIGHEST,
                     preferred_element_type=jnp.float32)
    energy = jnp.zeros((8, LANES), jnp.float32)
    for t in range(cols // LANES):
        energy = jnp.where(lane % pcol // 2 == t, halves[t * 8 : t * 8 + 8], energy)
    energy = energy / (PATCH * PATCH) + EPS

    pl.semaphore_wait(barrier, n)
    e0_copy = pltpu.make_async_remote_copy(
        src_ref=e0_v, dst_ref=e0_v, send_sem=e0_send, recv_sem=e0_recv,
        device_id=partner, device_id_type=MESH,
    )

    @pl.when(ch == 0)
    def _():
        e0_v[...] = energy
        e0_copy.start()

    @pl.when(ch == 1)
    def _():
        e0_copy.wait_recv()

    ref_energy = jnp.concatenate([e0_v[0:prow]] * chans, axis=0)
    weight = jnp.sqrt(ref_energy * energy)
    mine = sub // prow == lane // (2 * pcol)
    scaled = jnp.where((lane // pcol) % 2 == 1, weight * shift_v[1], weight)
    msg_v[0:1, :] = jnp.sum(jnp.where(mine, scaled, 0.0), axis=0, keepdims=True)
    first = lane < pcol
    w_rows = jnp.sum(jnp.where(first, weight, 0.0), axis=1, keepdims=True)
    ws_rows = jnp.sum(jnp.where(first, weight * shift_v[0], 0.0), axis=1, keepdims=True)
    base = lax.rem(ty, ty_block) * per_dev + sub // prow * per_chan + sub % prow
    spread = jnp.where(lane == base, w_rows, jnp.where(lane == base + prow, ws_rows, 0.0))
    msg_v[1:2, :] = jnp.sum(spread, axis=0, keepdims=True)
    slots_v[me, 0:2] = msg_v[0:2]

    def msg_copy(p, slot):
        _, where = peer_id(p)
        return pltpu.make_async_remote_copy(
            src_ref=msg_v.at[pl.ds(0, 2)], dst_ref=slots_v.at[slot, pl.ds(0, 2)],
            send_sem=msg_send.at[p], recv_sem=msg_recv.at[slot],
            device_id=where, device_id_type=MESH,
        )

    repeat_for(1, n, lambda p: msg_copy(p, me).start())

    span_y = {1: (rows - HY, 0, HY), -1: (0, HY + rows, HY), 0: (0, HY, rows)}
    span_x = {1: (cols - HX, 0, HX), -1: (0, HX + cols, HX), 0: (0, HX, cols)}
    sides = [(0, 1), (0, -1), (1, 0), (-1, 0), (1, 1), (1, -1), (-1, 1), (-1, -1)]
    halos, fills = [], []
    for s, (dy, dx) in enumerate(sides):
        sy, qy, ly = span_y[dy]
        sx, qx, lx = span_x[dx]
        dst = pad_hbm.at[:, pl.ds(qy, ly), pl.ds(qx, lx)]
        to_y, to_x = ty + dy, tx + dx
        from_y, from_x = ty - dy, tx - dx
        has_to = (to_y >= 0) & (to_y < n_ty) & (to_x >= 0) & (to_x < n_tx)
        has_from = (from_y >= 0) & (from_y < n_ty) & (from_x >= 0) & (from_x < n_tx)
        halo = pltpu.make_async_remote_copy(
            src_ref=img_v.at[:, pl.ds(sy, ly), pl.ds(sx, lx)], dst_ref=dst,
            send_sem=halo_send.at[s], recv_sem=halo_recv.at[s],
            device_id={"ty": to_y, "tx": to_x}, device_id_type=MESH,
        )
        zeros = zero_c if ly == rows else zero_r
        fill = pltpu.make_async_copy(
            zeros.at[:, pl.ds(0, ly), pl.ds(0, lx)], dst, zero_sem.at[s]
        )
        pl.when(has_to)(halo.start)
        pl.when(jnp.logical_not(has_from))(fill.start)
        halos.append((halo, has_to, has_from, fill))
    for own in owns:
        own.start()

    bases = {}
    for t in range(chunks):
        span = set()
        if t < n_tx:
            span |= set(range(t * per_x, t * per_x + per_x + 3))
        if t < blocks:
            span |= set(range(t * per_y, t * per_y + per_y + 3))
        for k in sorted(span):
            if k < keys:
                local = jnp.where(col_sys, col_pos + (t * per_x - k), row_pos + (t * per_y - k))
                bases[k, t] = bspline(local.astype(jnp.float32))

    def msg_wait(p):
        peer, _ = peer_id(p)
        msg_copy(p, peer).wait_recv()

    repeat_for(1, n, msg_wait)

    data_w, data_r = [], []
    for t in range(chunks):
        data = jnp.zeros((8, LANES), jnp.float32)
        if t < n_tx:
            total = slots_v[t, 0:1]
            for y in range(1, n_ty):
                total = total + slots_v[y * n_tx + t, 0:1]
            data = jnp.where(col_sys & (lane // (2 * pcol) == sub), total, data)
        if t < blocks:
            low, high = t * ty_block * n_tx, min(n_ty, (t + 1) * ty_block) * n_tx
            total = slots_v[low, 1:2]
            for y in range(low + 1, high):
                total = total + slots_v[y, 1:2]
            data = jnp.where(row_sys & (lane % per_dev // per_chan == sub - chans), total, data)
        data_w.append(jnp.where(is_rhs, 0.0, data))
        data_r.append(jnp.where(is_rhs, data, 0.0))

    pen_y, pen_x = penalty_band(key_y), penalty_band(key_x)

    def added(d, k):
        rest = 1.0 if d == 0 else 0.0
        at_x = lam_x * pen_x[d][k] if k < key_x else rest
        at_y = lam_y * pen_y[d][k] if k < key_y else rest
        if at_x == at_y == rest:
            return rest
        return jnp.where(col_sys, at_x, jnp.where(row_sys, at_y, rest))

    band, rhs = {}, []
    for k in range(keys):
        for d in range(4):
            if k + d >= keys:
                continue
            total = None
            for t in range(chunks):
                if (k, t) in bases and (k + d, t) in bases:
                    term = bases[k, t] * bases[k + d, t] * data_w[t]
                    total = term if total is None else total + term
            if total is None:
                band[k, d] = jnp.zeros((8, LANES), jnp.float32) + added(d, k)
            else:
                band[k, d] = jnp.broadcast_to(jnp.sum(total, axis=1, keepdims=True), (8, LANES)) + added(d, k)
        total = None
        for t in range(chunks):
            if (k, t) in bases:
                term = bases[k, t] * data_r[t]
                total = term if total is None else total + term
        rhs.append(jnp.broadcast_to(jnp.sum(total, axis=1, keepdims=True), (8, LANES)))

    recips = []
    for k in range(keys):
        recip = 1.0 / band[k, 0]
        recips.append(recip)
        for e in range(1, 4):
            if k + e >= keys:
                break
            factor = band[k, e] * recip
            for f in range(e, 4):
                if k + f < keys:
                    band[k + e, f - e] = band[k + e, f - e] - factor * band[k, f]
            rhs[k + e] = rhs[k + e] - factor * rhs[k]
    solved = [None] * keys
    for k in reversed(range(keys)):
        value = rhs[k]
        for e in range(3, 0, -1):
            if k + e < keys:
                value = value - band[k, e] * solved[k + e]
        solved[k] = value * recips[k]
        coef_v[k] = solved[k]

    lane_f = lane.astype(jnp.float32) + 0.5
    for out_ref, span, size, start, bound in (
        (col_ref, SPAN_X, cols, tx * (cols // SPAN_X), MAX_X),
        (row_ref, SPAN_Y, rows, ty * (rows // SPAN_Y), MAX_Y),
    ):
        tiles = span // LANES
        shape = [
            [bspline((lane_f + u * LANES) / span - e + 1.0) for e in range(4)] for u in range(tiles)
        ]
        for q in range(size // span):
            coefs = [coef_v[start + q + e] for e in range(4)]
            for u in range(tiles):
                total = coefs[0] * shape[u][0]
                for e in range(1, 4):
                    total = total + coefs[e] * shape[u][e]
                at = (q * tiles + u) * LANES
                out_ref[:, at : at + LANES] = bound * jnp.tanh(total / bound)

    for halo, has_to, has_from, fill in halos:
        pl.when(has_from)(halo.wait_recv)
        pl.when(jnp.logical_not(has_from))(fill.wait)
        pl.when(has_to)(halo.wait_send)
    for own in owns:
        own.wait()
    pl.when(ch == 0)(e0_copy.wait_send)
    repeat_for(1, n, lambda p: msg_copy(p, me).wait_send())


BLOCK = 256
HALF = 128
PAD = 64


def taps(target, depth, shift):
    low = jnp.floor(target)
    frac = target - low
    weights = [cubic_kernel(float(e) - frac).astype(jnp.bfloat16) for e in (-1, 0, 1, 2)]
    shape = (depth, target.shape[1])
    source = (lax.broadcasted_iota(jnp.int32, shape, 0) - shift).astype(jnp.float32).astype(jnp.bfloat16)
    offset = source - (low - shift).astype(jnp.bfloat16)
    out = jnp.zeros(shape, jnp.bfloat16)
    for e, weight in zip((-1, 0, 1, 2), weights):
        out = jnp.where(offset == e, jnp.broadcast_to(weight, shape), out)
    return out


def warp_kernel(pad_ref, col_ref, row_ref, out_hbm, rows_v, rtaps_v, ctaps_v, out_v, out_sem):
    chans, rows, cols = out_v.shape
    depth = pad_ref.shape[1]
    steps = cols // BLOCK
    lane_f = lax.broadcasted_iota(jnp.int32, (1, HALF), 1).astype(jnp.float32)
    row_f = lax.broadcasted_iota(jnp.int32, (1, rows), 1).astype(jnp.float32)
    for slot in range(2):
        ctaps_v[slot] = jnp.zeros(ctaps_v.shape[1:], jnp.bfloat16)
    for c in range(chans):
        target = row_f + HY + row_ref[chans + c : chans + c + 1, :]
        source = lax.broadcasted_iota(jnp.int32, (depth, rows), 0).astype(jnp.float32)
        rtaps_v[c] = cubic_kernel(source - target).T.astype(jnp.bfloat16)
    copies = []
    for c in range(chans):
        def row_tile(b):
            rows_v[c, :, b * BLOCK : (b + 1) * BLOCK] = jnp.dot(
                rtaps_v[c], pad_ref[c, :, b * BLOCK : (b + 1) * BLOCK],
                preferred_element_type=jnp.float32,
            ).astype(jnp.bfloat16)

        row_tile(0)
        for b in range(steps):
            row_tile(b + 1)
            slot = b % 2
            for h in range(BLOCK // HALF):
                at = b * BLOCK + h * HALF
                target = lane_f + float(PAD) + col_ref[c : c + 1, at : at + HALF]
                ctaps_v[slot, PAD + h * HALF : PAD + (h + 2) * HALF, h * HALF : (h + 1) * HALF] = (
                    taps(target, 2 * HALF, HALF)
                )
            out_v[c, :, b * BLOCK : (b + 1) * BLOCK] = jnp.dot(
                rows_v[c, :, b * BLOCK : (b + 2) * BLOCK], ctaps_v[slot],
                preferred_element_type=jnp.float32,
            ).astype(jnp.bfloat16)
            part = (c, slice(None), pl.ds(b * BLOCK, BLOCK))
            copy = pltpu.make_async_copy(out_v.at[part], out_hbm.at[part], out_sem.at[c * steps + b])
            copy.start()
            copies.append(copy)
    for copy in copies:
        copy.wait()


def local(image_plane, patch_shift):
    n_ty, n_tx = lax.axis_size("ty"), lax.axis_size("tx")
    chans, rows, cols = image_plane.shape
    n = n_ty * n_tx
    lam_y = SPAN_Y / PATCH * (cols * n_tx / PATCH) * (2.0 * rows / SPAN_Y) ** 4
    lam_x = SPAN_X / PATCH * (rows * n_ty / PATCH) * (1.0 * cols / SPAN_X) ** 4
    keys = max(n_ty * rows // SPAN_Y, n_tx * cols // SPAN_X) + 3
    high, wide = rows + 2 * HY, cols + 2 * HX
    f32 = jnp.float32
    dma = pltpu.SemaphoreType.DMA
    vmem = pl.BlockSpec(memory_space=pltpu.VMEM)
    hbm = pl.BlockSpec(memory_space=pltpu.HBM)
    padded, col_disp, row_disp = pl.pallas_call(
        functools.partial(fit_kernel, n_ty, n_tx, lam_y, lam_x),
        out_shape=(
            jax.ShapeDtypeStruct((chans, high, wide), jnp.bfloat16),
            jax.ShapeDtypeStruct((8, cols), f32),
            jax.ShapeDtypeStruct((8, rows), f32),
        ),
        in_specs=[hbm, hbm],
        out_specs=(pl.BlockSpec(memory_space=pltpu.VMEM), vmem, vmem),
        scratch_shapes=[
            pltpu.VMEM((chans, rows, cols), jnp.bfloat16),
            pltpu.VMEM(patch_shift.shape, jnp.int32),
            pltpu.VMEM((LANES, LANES), f32),
            pltpu.VMEM((2, 8, LANES), f32),
            pltpu.VMEM((8, LANES), f32),
            pltpu.VMEM((8, LANES), f32),
            pltpu.VMEM((n, 8, LANES), f32),
            pltpu.VMEM((keys, 8, LANES), f32),
            pltpu.VMEM((chans, HY, cols), jnp.bfloat16),
            pltpu.VMEM((chans, rows, HX), jnp.bfloat16),
            dma((8,)), dma, dma((chans,)), dma((8,)), dma, dma,
            dma((n,)), dma((n,)), dma((8,)), dma((8,)),
        ],
        compiler_params=pltpu.CompilerParams(
            collective_id=0, has_side_effects=True, vmem_limit_bytes=32 * 2**20
        ),
    )(image_plane, patch_shift)
    bf16 = jnp.bfloat16
    return pl.pallas_call(
        warp_kernel,
        out_shape=jax.ShapeDtypeStruct((chans, rows, cols), bf16),
        in_specs=[vmem, vmem, vmem],
        out_specs=hbm,
        scratch_shapes=[
            pltpu.VMEM((chans, rows, wide), bf16),
            pltpu.VMEM((chans, rows, high), bf16),
            pltpu.VMEM((2, 2 * BLOCK, BLOCK), bf16),
            pltpu.VMEM((chans, rows, cols), bf16),
            dma((chans * cols // BLOCK,)),
        ],
        compiler_params=pltpu.CompilerParams(vmem_limit_bytes=32 * 2**20),
    )(padded, col_disp, row_disp)


def solution(mesh):
    return jax.shard_map(
        local,
        mesh=mesh,
        in_specs=(P("ch", "ty", "tx"), P("ch", None, "ty", "tx")),
        out_specs=P("ch", "ty", "tx"),
        check_vma=False,
    )
```

```python
import functools

import jax
import jax.numpy as jnp
from jax import lax
from jax.experimental import pallas as pl
from jax.experimental.pallas import tpu as pltpu
from jax.sharding import PartitionSpec as P

PATCH = 64
SPAN_Y = 256
SPAN_X = 512
MAX_Y = 12
MAX_X = 60
HY = 16
HX = 64
EPS = 1e-05
LANES = 128
MESH = pl.DeviceIdType.MESH


def bspline(offset):
    mag = jnp.abs(offset)
    near_part = 2.0 / 3.0 - mag * mag + 0.5 * mag * mag * mag
    far_part = (2.0 - mag) * (2.0 - mag) * (2.0 - mag) / 6.0
    return jnp.where(mag < 1.0, near_part, jnp.where(mag < 2.0, far_part, 0.0))


def cubic_kernel(offset):
    a = jnp.maximum(2.0 - jnp.abs(offset), 0.0)
    c = a - 1.0
    b = jnp.maximum(c, 0.0)
    return a * a * (0.5 * c) + b * b * (1.0 - 2.0 * b)


def penalty_band(count):
    band = [[0.0] * count for _ in range(4)]
    coef = (1.0, -2.0, 1.0)
    for q in range(count - 2):
        for a in range(3):
            for b in range(a, 3):
                band[b - a][q + a] += coef[a] * coef[b]
    return band


def iota(dim, shape=(8, LANES)):
    return lax.broadcasted_iota(jnp.int32, shape, dim)


def repeat_for(start, stop, body):
    if stop - start <= 16:
        for i in range(start, stop):
            body(i)
    else:
        lax.fori_loop(start, stop, lambda i, _: (body(i), 0)[1], 0)


def fit_kernel(n_ty, n_tx, lam_y, lam_x, img_hbm, shift_hbm, main_hbm, side_hbm, col_ref, row_ref,
               img_v, shift_ref, sums_v, shift_v, e0_v, msg_v, slots_v, coef_v, pack_v, zero_v,
               img_sem, shift_sem, own_sem, zero_sem, e0_send, e0_recv, msg_send, msg_recv,
               halo_send, halo_recv):
    chans, rows, cols = img_v.shape
    prow, pcol = rows // PATCH, cols // PATCH
    n = n_ty * n_tx
    ch, ty, tx = lax.axis_index("ch"), lax.axis_index("ty"), lax.axis_index("tx")
    me = ty * n_tx + tx

    def peer_id(p):
        peer = lax.rem(me + p, n)
        return peer, {"ty": peer // n_tx, "tx": lax.rem(peer, n_tx)}

    barrier = pltpu.get_barrier_semaphore()
    partner = {"ch": 1 - ch}
    pl.semaphore_signal(barrier, inc=1, device_id=partner, device_id_type=MESH)

    def greet(p):
        _, where = peer_id(p)
        pl.semaphore_signal(barrier, inc=1, device_id=where, device_id_type=MESH)

    shift_load = pltpu.make_async_copy(shift_hbm, shift_ref, shift_sem)
    shift_load.start()
    loads = []
    for c in range(chans):
        for i in range(prow):
            copy = pltpu.make_async_copy(
                img_hbm.at[c, pl.ds(i * PATCH, PATCH)],
                img_v.at[c, pl.ds(i * PATCH, PATCH)],
                img_sem.at[c * prow + i],
            )
            copy.start()
            loads.append(copy)
    repeat_for(1, n, greet)
    zero_v[...] = jnp.zeros_like(zero_v)

    sub, lane = iota(0), iota(1)
    per_chan = 2 * prow
    per_dev = chans * per_chan
    ty_block = LANES // per_dev
    blocks = (n_ty + ty_block - 1) // ty_block
    col_sys = sub < chans
    row_sys = (sub >= chans) & (sub < 2 * chans)
    is_rhs = jnp.where(col_sys, (lane // pcol) % 2, (lane // prow) % 2) == 1
    key_y = n_ty * rows // SPAN_Y + 3
    key_x = n_tx * cols // SPAN_X + 3
    per_y, per_x = rows * ty_block // SPAN_Y, cols // SPAN_X
    keys = max(key_y, key_x)
    chunks = max(n_tx, blocks)
    col_pos = (lane % pcol * PATCH).astype(jnp.float32) / SPAN_X + (PATCH / 2.0 / SPAN_X + 1.0)
    row_index = lane // per_dev * prow + lane % prow
    row_pos = (row_index * PATCH).astype(jnp.float32) / SPAN_Y + (PATCH / 2.0 / SPAN_Y + 1.0)
    shift_load.wait()
    for q in range(2):
        for c in range(chans):
            part = shift_ref[c, q].astype(jnp.float32)
            for g in range(LANES // pcol):
                shift_v[q, pl.ds(c * prow, prow), pl.ds(g * pcol, pcol)] = part
    ind = (iota(0, (LANES, LANES)) // PATCH == iota(1, (LANES, LANES)) % 2).astype(jnp.float32)

    for c in range(chans):
        for i in range(prow):
            loads[c * prow + i].wait()
            for t in range(cols // LANES):
                part = img_v[c, pl.ds(i * PATCH, PATCH), pl.ds(t * LANES, LANES)].astype(jnp.float32)
                sums_v[pl.ds(t * 8 + c * prow + i, 1), :] = jnp.sum(part * part, axis=0, keepdims=True)
    owns = [
        pltpu.make_async_copy(
            img_v.at[c], main_hbm.at[c, pl.ds(HY, rows)], own_sem.at[c]
        )
        for c in range(chans)
    ]
    halves = jnp.dot(sums_v[...], ind, precision=lax.Precision.HIGHEST,
                     preferred_element_type=jnp.float32)
    energy = jnp.zeros((8, LANES), jnp.float32)
    for t in range(cols // LANES):
        energy = jnp.where(lane % pcol // 2 == t, halves[t * 8 : t * 8 + 8], energy)
    energy = energy / (PATCH * PATCH) + EPS

    pl.semaphore_wait(barrier, n)
    e0_copy = pltpu.make_async_remote_copy(
        src_ref=e0_v, dst_ref=e0_v, send_sem=e0_send, recv_sem=e0_recv,
        device_id=partner, device_id_type=MESH,
    )

    @pl.when(ch == 0)
    def _():
        e0_v[...] = energy
        e0_copy.start()

    @pl.when(ch == 1)
    def _():
        e0_copy.wait_recv()

    ref_energy = jnp.concatenate([e0_v[0:prow]] * chans, axis=0)
    weight = jnp.sqrt(ref_energy * energy)
    mine = sub // prow == lane // (2 * pcol)
    scaled = jnp.where((lane // pcol) % 2 == 1, weight * shift_v[1], weight)
    msg_v[0:1, :] = jnp.sum(jnp.where(mine, scaled, 0.0), axis=0, keepdims=True)
    first = lane < pcol
    w_rows = jnp.sum(jnp.where(first, weight, 0.0), axis=1, keepdims=True)
    ws_rows = jnp.sum(jnp.where(first, weight * shift_v[0], 0.0), axis=1, keepdims=True)
    base = lax.rem(ty, ty_block) * per_dev + sub // prow * per_chan + sub % prow
    spread = jnp.where(lane == base, w_rows, jnp.where(lane == base + prow, ws_rows, 0.0))
    msg_v[1:2, :] = jnp.sum(spread, axis=0, keepdims=True)
    slots_v[me, 0:2] = msg_v[0:2]

    def msg_copy(p, slot):
        _, where = peer_id(p)
        return pltpu.make_async_remote_copy(
            src_ref=msg_v.at[pl.ds(0, 2)], dst_ref=slots_v.at[slot, pl.ds(0, 2)],
            send_sem=msg_send.at[p], recv_sem=msg_recv.at[slot],
            device_id=where, device_id_type=MESH,
        )

    repeat_for(1, n, lambda p: msg_copy(p, me).start())

    tail, head = cols - 2 * HX, 2 * HX
    pack_v[0] = jnp.concatenate([img_v[0, :, tail + HX :], img_v[1, :, tail + HX :]], axis=1)
    pack_v[1] = jnp.concatenate([img_v[0, :, :HX], img_v[1, :, :HX]], axis=1)
    span_y = {1: (rows - HY, 0, HY), -1: (0, HY + rows, HY), 0: (0, HY, rows)}
    sides = [(0, 1), (0, -1), (1, 0), (-1, 0), (1, 1), (1, -1), (-1, 1), (-1, -1)]
    halos = []
    for s, (dy, dx) in enumerate(sides):
        sy, qy, ly = span_y[dy]
        if dx == 0:
            src, dst = img_v.at[:, pl.ds(sy, ly)], main_hbm.at[:, pl.ds(qy, ly)]
            zeros = zero_v.at[:, pl.ds(0, ly)]
        else:
            side = 0 if dx == 1 else 1
            src, dst = pack_v.at[side, pl.ds(sy, ly)], side_hbm.at[side, pl.ds(qy, ly)]
            zeros = zero_v.at[0, pl.ds(0, ly), pl.ds(0, head)]
        to_y, to_x = ty + dy, tx + dx
        from_y, from_x = ty - dy, tx - dx
        has_to = (to_y >= 0) & (to_y < n_ty) & (to_x >= 0) & (to_x < n_tx)
        has_from = (from_y >= 0) & (from_y < n_ty) & (from_x >= 0) & (from_x < n_tx)
        halo = pltpu.make_async_remote_copy(
            src_ref=src, dst_ref=dst, send_sem=halo_send.at[s], recv_sem=halo_recv.at[s],
            device_id={"ty": to_y, "tx": to_x}, device_id_type=MESH,
        )
        fill = pltpu.make_async_copy(zeros, dst, zero_sem.at[s])
        pl.when(has_to)(halo.start)
        pl.when(jnp.logical_not(has_from))(fill.start)
        halos.append((halo, has_to, has_from, fill))
    for own in owns:
        own.start()

    bases = {}
    for t in range(chunks):
        span = set()
        if t < n_tx:
            span |= set(range(t * per_x, t * per_x + per_x + 3))
        if t < blocks:
            span |= set(range(t * per_y, t * per_y + per_y + 3))
        for k in sorted(span):
            if k < keys:
                local = jnp.where(col_sys, col_pos + (t * per_x - k), row_pos + (t * per_y - k))
                bases[k, t] = bspline(local.astype(jnp.float32))

    def msg_wait(p):
        peer, _ = peer_id(p)
        msg_copy(p, peer).wait_recv()

    repeat_for(1, n, msg_wait)

    data_w, data_r = [], []
    for t in range(chunks):
        data = jnp.zeros((8, LANES), jnp.float32)
        if t < n_tx:
            total = slots_v[t, 0:1]
            for y in range(1, n_ty):
                total = total + slots_v[y * n_tx + t, 0:1]
            data = jnp.where(col_sys & (lane // (2 * pcol) == sub), total, data)
        if t < blocks:
            low, high = t * ty_block * n_tx, min(n_ty, (t + 1) * ty_block) * n_tx
            total = slots_v[low, 1:2]
            for y in range(low + 1, high):
                total = total + slots_v[y, 1:2]
            data = jnp.where(row_sys & (lane % per_dev // per_chan == sub - chans), total, data)
        data_w.append(jnp.where(is_rhs, 0.0, data))
        data_r.append(jnp.where(is_rhs, data, 0.0))

    pen_y, pen_x = penalty_band(key_y), penalty_band(key_x)

    def added(d, k):
        rest = 1.0 if d == 0 else 0.0
        at_x = lam_x * pen_x[d][k] if k < key_x else rest
        at_y = lam_y * pen_y[d][k] if k < key_y else rest
        if at_x == at_y == rest:
            return rest
        return jnp.where(col_sys, at_x, jnp.where(row_sys, at_y, rest))

    band, rhs = {}, []
    for k in range(keys):
        for d in range(4):
            if k + d >= keys:
                continue
            total = None
            for t in range(chunks):
                if (k, t) in bases and (k + d, t) in bases:
                    term = bases[k, t] * bases[k + d, t] * data_w[t]
                    total = term if total is None else total + term
            if total is None:
                band[k, d] = jnp.zeros((8, LANES), jnp.float32) + added(d, k)
            else:
                band[k, d] = jnp.broadcast_to(jnp.sum(total, axis=1, keepdims=True), (8, LANES)) + added(d, k)
        total = None
        for t in range(chunks):
            if (k, t) in bases:
                term = bases[k, t] * data_r[t]
                total = term if total is None else total + term
        rhs.append(jnp.broadcast_to(jnp.sum(total, axis=1, keepdims=True), (8, LANES)))

    recips = []
    for k in range(keys):
        recip = 1.0 / band[k, 0]
        recips.append(recip)
        for e in range(1, 4):
            if k + e >= keys:
                break
            factor = band[k, e] * recip
            for f in range(e, 4):
                if k + f < keys:
                    band[k + e, f - e] = band[k + e, f - e] - factor * band[k, f]
            rhs[k + e] = rhs[k + e] - factor * rhs[k]
    solved = [None] * keys
    for k in reversed(range(keys)):
        value = rhs[k]
        for e in range(3, 0, -1):
            if k + e < keys:
                value = value - band[k, e] * solved[k + e]
        solved[k] = value * recips[k]
        coef_v[k] = solved[k]

    lane_f = lane.astype(jnp.float32) + 0.5
    for out_ref, span, size, start, bound in (
        (col_ref, SPAN_X, cols, tx * (cols // SPAN_X), MAX_X),
        (row_ref, SPAN_Y, rows, ty * (rows // SPAN_Y), MAX_Y),
    ):
        tiles = span // LANES
        shape = [
            [bspline((lane_f + u * LANES) / span - e + 1.0) for e in range(4)] for u in range(tiles)
        ]
        for q in range(size // span):
            coefs = [coef_v[start + q + e] for e in range(4)]
            for u in range(tiles):
                total = coefs[0] * shape[u][0]
                for e in range(1, 4):
                    total = total + coefs[e] * shape[u][e]
                at = (q * tiles + u) * LANES
                out_ref[:, at : at + LANES] = bound * jnp.tanh(total / bound)

    for halo, has_to, has_from, fill in halos:
        pl.when(has_from)(halo.wait_recv)
        pl.when(jnp.logical_not(has_from))(fill.wait)
        pl.when(has_to)(halo.wait_send)
    for own in owns:
        own.wait()
    pl.when(ch == 0)(e0_copy.wait_send)
    repeat_for(1, n, lambda p: msg_copy(p, me).wait_send())


BLOCK = 256
HALF = 128
PAD = 64


def taps(target, depth, shift):
    low = jnp.floor(target)
    frac = target - low
    weights = [cubic_kernel(float(e) - frac).astype(jnp.bfloat16) for e in (-1, 0, 1, 2)]
    shape = (depth, target.shape[1])
    source = (lax.broadcasted_iota(jnp.int32, shape, 0) - shift).astype(jnp.float32).astype(jnp.bfloat16)
    offset = source - (low - shift).astype(jnp.bfloat16)
    out = jnp.zeros(shape, jnp.bfloat16)
    for e, weight in zip((-1, 0, 1, 2), weights):
        out = jnp.where(offset == e, jnp.broadcast_to(weight, shape), out)
    return out


def warp_kernel(main_hbm, side_hbm, col_hbm, row_hbm, out_hbm, pad_ref, side_v, col_ref, row_ref,
                rows_v, rtaps_v, ctaps_v, out_v, out_sem, in_sem, small_sem):
    chans, rows, cols = out_v.shape
    depth = pad_ref.shape[1]
    steps = cols // BLOCK
    edge = 2 * HX
    small = [
        pltpu.make_async_copy(row_hbm, row_ref, small_sem.at[0]),
        pltpu.make_async_copy(side_hbm, side_v, small_sem.at[1]),
        pltpu.make_async_copy(col_hbm, col_ref, small_sem.at[2]),
    ]
    loads = [
        pltpu.make_async_copy(
            main_hbm.at[c, :, pl.ds(b * BLOCK, BLOCK)],
            pad_ref.at[c, :, pl.ds(edge + b * BLOCK, BLOCK)],
            in_sem.at[c * steps + b],
        )
        for c in range(chans) for b in range(steps)
    ]
    small[0].start()
    small[1].start()
    loads[0].start()
    small[2].start()
    for load in loads[1:]:
        load.start()
    lane_f = lax.broadcasted_iota(jnp.int32, (1, HALF), 1).astype(jnp.float32)
    row_f = lax.broadcasted_iota(jnp.int32, (1, rows), 1).astype(jnp.float32)
    for slot in range(2):
        ctaps_v[slot] = jnp.zeros(ctaps_v.shape[1:], jnp.bfloat16)
    small[0].wait()
    for c in range(chans):
        target = row_f + HY + row_ref[chans + c : chans + c + 1, :]
        source = lax.broadcasted_iota(jnp.int32, (depth, rows), 0).astype(jnp.float32)
        rtaps_v[c] = cubic_kernel(source - target).T.astype(jnp.bfloat16)
    small[1].wait()
    for i in range(2):
        whole = side_v[i]
        other = jnp.concatenate([whole[:, HX:], whole[:, :HX]], axis=1)
        at = 0 if i == 0 else edge + cols
        pad_ref[i, :, at : at + edge] = other
        pad_ref[1 - i, :, at : at + edge] = whole
    copies = []
    for c in range(chans):
        def row_tile(b):
            if b < steps:
                loads[c * steps + b].wait()
            rows_v[c, :, b * BLOCK : (b + 1) * BLOCK] = jnp.dot(
                rtaps_v[c], pad_ref[c, :, b * BLOCK : (b + 1) * BLOCK],
                preferred_element_type=jnp.float32,
            ).astype(jnp.bfloat16)

        small[2].wait() if c == 0 else None
        row_tile(0)
        for b in range(steps):
            row_tile(b + 1)
            slot = b % 2
            for h in range(BLOCK // HALF):
                at = b * BLOCK + h * HALF
                target = lane_f + float(PAD) + col_ref[c : c + 1, at : at + HALF]
                ctaps_v[slot, PAD + h * HALF : PAD + (h + 2) * HALF, h * HALF : (h + 1) * HALF] = (
                    taps(target, 2 * HALF, HALF)
                )
            out_v[c, :, b * BLOCK : (b + 1) * BLOCK] = jnp.dot(
                rows_v[c, :, b * BLOCK : (b + 2) * BLOCK], ctaps_v[slot],
                preferred_element_type=jnp.float32,
            ).astype(jnp.bfloat16)
            part = (c, slice(None), pl.ds(b * BLOCK, BLOCK))
            copy = pltpu.make_async_copy(out_v.at[part], out_hbm.at[part], out_sem.at[c * steps + b])
            copy.start()
            copies.append(copy)
    for copy in copies:
        copy.wait()


def local(image_plane, patch_shift):
    n_ty, n_tx = lax.axis_size("ty"), lax.axis_size("tx")
    chans, rows, cols = image_plane.shape
    n = n_ty * n_tx
    lam_y = SPAN_Y / PATCH * (cols * n_tx / PATCH) * (2.0 * rows / SPAN_Y) ** 4
    lam_x = SPAN_X / PATCH * (rows * n_ty / PATCH) * (1.0 * cols / SPAN_X) ** 4
    keys = max(n_ty * rows // SPAN_Y, n_tx * cols // SPAN_X) + 3
    high, wide = rows + 2 * HY, cols + 4 * HX
    f32 = jnp.float32
    dma = pltpu.SemaphoreType.DMA
    vmem = pl.BlockSpec(memory_space=pltpu.VMEM)
    hbm = pl.BlockSpec(memory_space=pltpu.HBM)
    main, side, col_disp, row_disp = pl.pallas_call(
        functools.partial(fit_kernel, n_ty, n_tx, lam_y, lam_x),
        out_shape=(
            jax.ShapeDtypeStruct((chans, high, cols), jnp.bfloat16),
            jax.ShapeDtypeStruct((2, high, 2 * HX), jnp.bfloat16),
            jax.ShapeDtypeStruct((8, cols), f32),
            jax.ShapeDtypeStruct((8, rows), f32),
        ),
        in_specs=[hbm, hbm],
        out_specs=(hbm, hbm, vmem, vmem),
        scratch_shapes=[
            pltpu.VMEM((chans, rows, cols), jnp.bfloat16),
            pltpu.VMEM(patch_shift.shape, jnp.int32),
            pltpu.VMEM((LANES, LANES), f32),
            pltpu.VMEM((2, 8, LANES), f32),
            pltpu.VMEM((8, LANES), f32),
            pltpu.VMEM((8, LANES), f32),
            pltpu.VMEM((n, 8, LANES), f32),
            pltpu.VMEM((keys, 8, LANES), f32),
            pltpu.VMEM((2, rows, 2 * HX), jnp.bfloat16),
            pltpu.VMEM((chans, rows, cols), jnp.bfloat16),
            dma((8,)), dma, dma((chans,)), dma((8,)), dma, dma,
            dma((n,)), dma((n,)), dma((8,)), dma((8,)),
        ],
        compiler_params=pltpu.CompilerParams(
            collective_id=0, has_side_effects=True, vmem_limit_bytes=58 * 2**20
        ),
    )(image_plane, patch_shift)
    bf16 = jnp.bfloat16
    return pl.pallas_call(
        warp_kernel,
        out_shape=jax.ShapeDtypeStruct((chans, rows, cols), bf16),
        in_specs=[hbm, hbm, hbm, hbm],
        out_specs=hbm,
        scratch_shapes=[
            pltpu.VMEM((chans, high, wide), bf16),
            pltpu.VMEM((2, high, 2 * HX), bf16),
            pltpu.VMEM((8, cols), f32),
            pltpu.VMEM((8, rows), f32),
            pltpu.VMEM((chans, rows, wide), bf16),
            pltpu.VMEM((chans, rows, high), bf16),
            pltpu.VMEM((2, 2 * BLOCK, BLOCK), bf16),
            pltpu.VMEM((chans, rows, cols), bf16),
            dma((chans * cols // BLOCK,)), dma((chans * cols // BLOCK,)), dma((3,)),
        ],
        compiler_params=pltpu.CompilerParams(vmem_limit_bytes=58 * 2**20),
    )(main, side, col_disp, row_disp)


def solution(mesh):
    return jax.shard_map(
        local,
        mesh=mesh,
        in_specs=(P("ch", "ty", "tx"), P("ch", None, "ty", "tx")),
        out_specs=P("ch", "ty", "tx"),
        check_vma=False,
    )
```

```python
import functools

import jax
import jax.numpy as jnp
from jax import lax
from jax.experimental import pallas as pl
from jax.experimental.pallas import tpu as pltpu
from jax.sharding import PartitionSpec as P

PATCH = 64
SPAN_Y = 256
SPAN_X = 512
MAX_Y = 12
MAX_X = 60
HY = 16
HX = 64
EPS = 1e-05
LANES = 128
MESH = pl.DeviceIdType.MESH


def bspline(offset):
    mag = jnp.abs(offset)
    near_part = 2.0 / 3.0 - mag * mag + 0.5 * mag * mag * mag
    far_part = (2.0 - mag) * (2.0 - mag) * (2.0 - mag) / 6.0
    return jnp.where(mag < 1.0, near_part, jnp.where(mag < 2.0, far_part, 0.0))


def cubic_kernel(offset):
    a = jnp.maximum(2.0 - jnp.abs(offset), 0.0)
    c = a - 1.0
    b = jnp.maximum(c, 0.0)
    return a * a * (0.5 * c) + b * b * (1.0 - 2.0 * b)


def penalty_band(count):
    band = [[0.0] * count for _ in range(4)]
    coef = (1.0, -2.0, 1.0)
    for q in range(count - 2):
        for a in range(3):
            for b in range(a, 3):
                band[b - a][q + a] += coef[a] * coef[b]
    return band


def iota(dim, shape=(8, LANES)):
    return lax.broadcasted_iota(jnp.int32, shape, dim)


def repeat_for(start, stop, body):
    if stop - start <= 16:
        for i in range(start, stop):
            body(i)
    else:
        lax.fori_loop(start, stop, lambda i, _: (body(i), 0)[1], 0)


def fit_kernel(n_ty, n_tx, lam_y, lam_x, img_v, shift_ref, pad_ref, col_ref, row_ref,
               side_v, sums_v, shift_v, e0_v, msg_v, slots_v, coef_v, pack_v, zero_v,
               own_sem, zero_sem, e0_send, e0_recv, msg_send, msg_recv,
               halo_send, halo_recv):
    chans, rows, cols = img_v.shape
    prow, pcol = rows // PATCH, cols // PATCH
    n = n_ty * n_tx
    ch, ty, tx = lax.axis_index("ch"), lax.axis_index("ty"), lax.axis_index("tx")
    me = ty * n_tx + tx

    def peer_id(p):
        peer = lax.rem(me + p, n)
        return peer, {"ty": peer // n_tx, "tx": lax.rem(peer, n_tx)}

    barrier = pltpu.get_barrier_semaphore()
    partner = {"ch": 1 - ch}
    pl.semaphore_signal(barrier, inc=1, device_id=partner, device_id_type=MESH)

    def greet(p):
        _, where = peer_id(p)
        pl.semaphore_signal(barrier, inc=1, device_id=where, device_id_type=MESH)

    repeat_for(1, n, greet)
    zero_v[...] = jnp.zeros_like(zero_v)

    sub, lane = iota(0), iota(1)
    per_chan = 2 * prow
    per_dev = chans * per_chan
    ty_block = LANES // per_dev
    blocks = (n_ty + ty_block - 1) // ty_block
    col_sys = sub < chans
    row_sys = (sub >= chans) & (sub < 2 * chans)
    is_rhs = jnp.where(col_sys, (lane // pcol) % 2, (lane // prow) % 2) == 1
    key_y = n_ty * rows // SPAN_Y + 3
    key_x = n_tx * cols // SPAN_X + 3
    per_y, per_x = rows * ty_block // SPAN_Y, cols // SPAN_X
    keys = max(key_y, key_x)
    chunks = max(n_tx, blocks)
    col_pos = (lane % pcol * PATCH).astype(jnp.float32) / SPAN_X + (PATCH / 2.0 / SPAN_X + 1.0)
    row_index = lane // per_dev * prow + lane % prow
    row_pos = (row_index * PATCH).astype(jnp.float32) / SPAN_Y + (PATCH / 2.0 / SPAN_Y + 1.0)
    for q in range(2):
        for c in range(chans):
            part = shift_ref[c, q].astype(jnp.float32)
            for g in range(LANES // pcol):
                shift_v[q, pl.ds(c * prow, prow), pl.ds(g * pcol, pcol)] = part
    ind = (iota(0, (LANES, LANES)) // PATCH == iota(1, (LANES, LANES)) % 2).astype(jnp.float32)

    for c in range(chans):
        for i in range(prow):
            for t in range(cols // LANES):
                part = img_v[c, pl.ds(i * PATCH, PATCH), pl.ds(t * LANES, LANES)].astype(jnp.float32)
                sums_v[pl.ds(t * 8 + c * prow + i, 1), :] = jnp.sum(part * part, axis=0, keepdims=True)
    owns = [
        pltpu.make_async_copy(
            img_v.at[c], pad_ref.at[c, pl.ds(HY, rows), pl.ds(2 * HX, cols)], own_sem.at[c]
        )
        for c in range(chans)
    ]
    halves = jnp.dot(sums_v[...], ind, precision=lax.Precision.HIGHEST,
                     preferred_element_type=jnp.float32)
    energy = jnp.zeros((8, LANES), jnp.float32)
    for t in range(cols // LANES):
        energy = jnp.where(lane % pcol // 2 == t, halves[t * 8 : t * 8 + 8], energy)
    energy = energy / (PATCH * PATCH) + EPS

    pl.semaphore_wait(barrier, n)
    e0_copy = pltpu.make_async_remote_copy(
        src_ref=e0_v, dst_ref=e0_v, send_sem=e0_send, recv_sem=e0_recv,
        device_id=partner, device_id_type=MESH,
    )

    @pl.when(ch == 0)
    def _():
        e0_v[...] = energy
        e0_copy.start()

    @pl.when(ch == 1)
    def _():
        e0_copy.wait_recv()

    ref_energy = jnp.concatenate([e0_v[0:prow]] * chans, axis=0)
    weight = jnp.sqrt(ref_energy * energy)
    mine = sub // prow == lane // (2 * pcol)
    scaled = jnp.where((lane // pcol) % 2 == 1, weight * shift_v[1], weight)
    msg_v[0:1, :] = jnp.sum(jnp.where(mine, scaled, 0.0), axis=0, keepdims=True)
    first = lane < pcol
    w_rows = jnp.sum(jnp.where(first, weight, 0.0), axis=1, keepdims=True)
    ws_rows = jnp.sum(jnp.where(first, weight * shift_v[0], 0.0), axis=1, keepdims=True)
    base = lax.rem(ty, ty_block) * per_dev + sub // prow * per_chan + sub % prow
    spread = jnp.where(lane == base, w_rows, jnp.where(lane == base + prow, ws_rows, 0.0))
    msg_v[1:2, :] = jnp.sum(spread, axis=0, keepdims=True)
    slots_v[me, 0:2] = msg_v[0:2]

    def msg_copy(p, slot):
        _, where = peer_id(p)
        return pltpu.make_async_remote_copy(
            src_ref=msg_v.at[pl.ds(0, 2)], dst_ref=slots_v.at[slot, pl.ds(0, 2)],
            send_sem=msg_send.at[p], recv_sem=msg_recv.at[slot],
            device_id=where, device_id_type=MESH,
        )

    repeat_for(1, n, lambda p: msg_copy(p, me).start())

    tail, head = cols - 2 * HX, 2 * HX
    pack_v[0] = jnp.concatenate([img_v[0, :, tail + HX :], img_v[1, :, tail + HX :]], axis=1)
    pack_v[1] = jnp.concatenate([img_v[0, :, :HX], img_v[1, :, :HX]], axis=1)
    span_y = {1: (rows - HY, 0, HY), -1: (0, HY + rows, HY), 0: (0, HY, rows)}
    sides = [(0, 1), (0, -1), (1, 0), (-1, 0), (1, 1), (1, -1), (-1, 1), (-1, -1)]
    halos = []
    for s, (dy, dx) in enumerate(sides):
        sy, qy, ly = span_y[dy]
        if dx == 0:
            src, dst = img_v.at[:, pl.ds(sy, ly)], pad_ref.at[:, pl.ds(qy, ly), pl.ds(2 * HX, cols)]
            zeros = zero_v.at[:, pl.ds(0, ly)]
        else:
            side = 0 if dx == 1 else 1
            src, dst = pack_v.at[side, pl.ds(sy, ly)], side_v.at[side, pl.ds(qy, ly)]
            zeros = zero_v.at[0, pl.ds(0, ly), pl.ds(0, head)]
        to_y, to_x = ty + dy, tx + dx
        from_y, from_x = ty - dy, tx - dx
        has_to = (to_y >= 0) & (to_y < n_ty) & (to_x >= 0) & (to_x < n_tx)
        has_from = (from_y >= 0) & (from_y < n_ty) & (from_x >= 0) & (from_x < n_tx)
        halo = pltpu.make_async_remote_copy(
            src_ref=src, dst_ref=dst, send_sem=halo_send.at[s], recv_sem=halo_recv.at[s],
            device_id={"ty": to_y, "tx": to_x}, device_id_type=MESH,
        )
        fill = pltpu.make_async_copy(zeros, dst, zero_sem.at[s])
        pl.when(has_to)(halo.start)
        pl.when(jnp.logical_not(has_from))(fill.start)
        halos.append((halo, has_to, has_from, fill))
    for own in owns:
        own.start()

    bases = {}
    for t in range(chunks):
        span = set()
        if t < n_tx:
            span |= set(range(t * per_x, t * per_x + per_x + 3))
        if t < blocks:
            span |= set(range(t * per_y, t * per_y + per_y + 3))
        for k in sorted(span):
            if k < keys:
                local = jnp.where(col_sys, col_pos + (t * per_x - k), row_pos + (t * per_y - k))
                bases[k, t] = bspline(local.astype(jnp.float32))

    def msg_wait(p):
        peer, _ = peer_id(p)
        msg_copy(p, peer).wait_recv()

    repeat_for(1, n, msg_wait)

    data_w, data_r = [], []
    for t in range(chunks):
        data = jnp.zeros((8, LANES), jnp.float32)
        if t < n_tx:
            total = slots_v[t, 0:1]
            for y in range(1, n_ty):
                total = total + slots_v[y * n_tx + t, 0:1]
            data = jnp.where(col_sys & (lane // (2 * pcol) == sub), total, data)
        if t < blocks:
            low, high = t * ty_block * n_tx, min(n_ty, (t + 1) * ty_block) * n_tx
            total = slots_v[low, 1:2]
            for y in range(low + 1, high):
                total = total + slots_v[y, 1:2]
            data = jnp.where(row_sys & (lane % per_dev // per_chan == sub - chans), total, data)
        data_w.append(jnp.where(is_rhs, 0.0, data))
        data_r.append(jnp.where(is_rhs, data, 0.0))

    pen_y, pen_x = penalty_band(key_y), penalty_band(key_x)

    def added(d, k):
        rest = 1.0 if d == 0 else 0.0
        at_x = lam_x * pen_x[d][k] if k < key_x else rest
        at_y = lam_y * pen_y[d][k] if k < key_y else rest
        if at_x == at_y == rest:
            return rest
        return jnp.where(col_sys, at_x, jnp.where(row_sys, at_y, rest))

    band, rhs = {}, []
    for k in range(keys):
        for d in range(4):
            if k + d >= keys:
                continue
            total = None
            for t in range(chunks):
                if (k, t) in bases and (k + d, t) in bases:
                    term = bases[k, t] * bases[k + d, t] * data_w[t]
                    total = term if total is None else total + term
            if total is None:
                band[k, d] = jnp.zeros((8, LANES), jnp.float32) + added(d, k)
            else:
                band[k, d] = jnp.broadcast_to(jnp.sum(total, axis=1, keepdims=True), (8, LANES)) + added(d, k)
        total = None
        for t in range(chunks):
            if (k, t) in bases:
                term = bases[k, t] * data_r[t]
                total = term if total is None else total + term
        rhs.append(jnp.broadcast_to(jnp.sum(total, axis=1, keepdims=True), (8, LANES)))

    recips = []
    for k in range(keys):
        recip = 1.0 / band[k, 0]
        recips.append(recip)
        for e in range(1, 4):
            if k + e >= keys:
                break
            factor = band[k, e] * recip
            for f in range(e, 4):
                if k + f < keys:
                    band[k + e, f - e] = band[k + e, f - e] - factor * band[k, f]
            rhs[k + e] = rhs[k + e] - factor * rhs[k]
    solved = [None] * keys
    for k in reversed(range(keys)):
        value = rhs[k]
        for e in range(3, 0, -1):
            if k + e < keys:
                value = value - band[k, e] * solved[k + e]
        solved[k] = value * recips[k]
        coef_v[k] = solved[k]

    lane_f = lane.astype(jnp.float32) + 0.5
    for out_ref, span, size, start, bound in (
        (col_ref, SPAN_X, cols, tx * (cols // SPAN_X), MAX_X),
        (row_ref, SPAN_Y, rows, ty * (rows // SPAN_Y), MAX_Y),
    ):
        tiles = span // LANES
        shape = [
            [bspline((lane_f + u * LANES) / span - e + 1.0) for e in range(4)] for u in range(tiles)
        ]
        for q in range(size // span):
            coefs = [coef_v[start + q + e] for e in range(4)]
            for u in range(tiles):
                total = coefs[0] * shape[u][0]
                for e in range(1, 4):
                    total = total + coefs[e] * shape[u][e]
                at = (q * tiles + u) * LANES
                out_ref[:, at : at + LANES] = bound * jnp.tanh(total / bound)

    for halo, has_to, has_from, fill in halos:
        pl.when(has_from)(halo.wait_recv)
        pl.when(jnp.logical_not(has_from))(fill.wait)
        pl.when(has_to)(halo.wait_send)
    for i in range(2):
        whole = side_v[i]
        other = jnp.concatenate([whole[:, HX:], whole[:, :HX]], axis=1)
        at = 0 if i == 0 else head + cols
        pad_ref[i, :, at : at + head] = other
        pad_ref[1 - i, :, at : at + head] = whole
    for own in owns:
        own.wait()
    pl.when(ch == 0)(e0_copy.wait_send)
    repeat_for(1, n, lambda p: msg_copy(p, me).wait_send())


BLOCK = 256
HALF = 128
PAD = 64


def taps(target, depth, shift):
    low = jnp.floor(target)
    frac = target - low
    weights = [cubic_kernel(float(e) - frac).astype(jnp.bfloat16) for e in (-1, 0, 1, 2)]
    shape = (depth, target.shape[1])
    source = (lax.broadcasted_iota(jnp.int32, shape, 0) - shift).astype(jnp.float32).astype(jnp.bfloat16)
    offset = source - (low - shift).astype(jnp.bfloat16)
    out = jnp.zeros(shape, jnp.bfloat16)
    for e, weight in zip((-1, 0, 1, 2), weights):
        out = jnp.where(offset == e, jnp.broadcast_to(weight, shape), out)
    return out


def warp_kernel(pad_ref, col_ref, row_ref, out_hbm, rows_v, rtaps_v, ctaps_v, out_v, out_sem):
    chans, rows, cols = out_v.shape
    depth = pad_ref.shape[1]
    steps = cols // BLOCK
    lane_f = lax.broadcasted_iota(jnp.int32, (1, HALF), 1).astype(jnp.float32)
    row_f = lax.broadcasted_iota(jnp.int32, (1, rows), 1).astype(jnp.float32)
    for slot in range(2):
        ctaps_v[slot] = jnp.zeros(ctaps_v.shape[1:], jnp.bfloat16)
    for c in range(chans):
        target = row_f + HY + row_ref[chans + c : chans + c + 1, :]
        source = lax.broadcasted_iota(jnp.int32, (depth, rows), 0).astype(jnp.float32)
        rtaps_v[c] = cubic_kernel(source - target).T.astype(jnp.bfloat16)
    copies = []
    for c in range(chans):
        def row_tile(b):
            rows_v[c, :, b * BLOCK : (b + 1) * BLOCK] = jnp.dot(
                rtaps_v[c], pad_ref[c, :, b * BLOCK : (b + 1) * BLOCK],
                preferred_element_type=jnp.float32,
            ).astype(jnp.bfloat16)

        row_tile(0)
        for b in range(steps):
            row_tile(b + 1)
            slot = b % 2
            for h in range(BLOCK // HALF):
                at = b * BLOCK + h * HALF
                target = lane_f + float(PAD) + col_ref[c : c + 1, at : at + HALF]
                ctaps_v[slot, PAD + h * HALF : PAD + (h + 2) * HALF, h * HALF : (h + 1) * HALF] = (
                    taps(target, 2 * HALF, HALF)
                )
            out_v[c, :, b * BLOCK : (b + 1) * BLOCK] = jnp.dot(
                rows_v[c, :, b * BLOCK : (b + 2) * BLOCK], ctaps_v[slot],
                preferred_element_type=jnp.float32,
            ).astype(jnp.bfloat16)
            part = (c, slice(None), pl.ds(b * BLOCK, BLOCK))
            copy = pltpu.make_async_copy(out_v.at[part], out_hbm.at[part], out_sem.at[c * steps + b])
            copy.start()
            copies.append(copy)
    for copy in copies:
        copy.wait()


def local(image_plane, patch_shift):
    n_ty, n_tx = lax.axis_size("ty"), lax.axis_size("tx")
    chans, rows, cols = image_plane.shape
    n = n_ty * n_tx
    lam_y = SPAN_Y / PATCH * (cols * n_tx / PATCH) * (2.0 * rows / SPAN_Y) ** 4
    lam_x = SPAN_X / PATCH * (rows * n_ty / PATCH) * (1.0 * cols / SPAN_X) ** 4
    keys = max(n_ty * rows // SPAN_Y, n_tx * cols // SPAN_X) + 3
    high, wide = rows + 2 * HY, cols + 4 * HX
    f32 = jnp.float32
    dma = pltpu.SemaphoreType.DMA
    vmem = pl.BlockSpec(memory_space=pltpu.VMEM)
    hbm = pl.BlockSpec(memory_space=pltpu.HBM)
    padded, col_disp, row_disp = pl.pallas_call(
        functools.partial(fit_kernel, n_ty, n_tx, lam_y, lam_x),
        out_shape=(
            jax.ShapeDtypeStruct((chans, high, wide), jnp.bfloat16),
            jax.ShapeDtypeStruct((8, cols), f32),
            jax.ShapeDtypeStruct((8, rows), f32),
        ),
        in_specs=[vmem, vmem],
        out_specs=(vmem, vmem, vmem),
        scratch_shapes=[
            pltpu.VMEM((2, high, 2 * HX), jnp.bfloat16),
            pltpu.VMEM((LANES, LANES), f32),
            pltpu.VMEM((2, 8, LANES), f32),
            pltpu.VMEM((8, LANES), f32),
            pltpu.VMEM((8, LANES), f32),
            pltpu.VMEM((n, 8, LANES), f32),
            pltpu.VMEM((keys, 8, LANES), f32),
            pltpu.VMEM((2, rows, 2 * HX), jnp.bfloat16),
            pltpu.VMEM((chans, rows, cols), jnp.bfloat16),
            dma((chans,)), dma((8,)), dma, dma,
            dma((n,)), dma((n,)), dma((8,)), dma((8,)),
        ],
        compiler_params=pltpu.CompilerParams(
            collective_id=0, has_side_effects=True, vmem_limit_bytes=32 * 2**20
        ),
    )(image_plane, patch_shift)
    bf16 = jnp.bfloat16
    return pl.pallas_call(
        warp_kernel,
        out_shape=jax.ShapeDtypeStruct((chans, rows, cols), bf16),
        in_specs=[vmem, vmem, vmem],
        out_specs=hbm,
        scratch_shapes=[
            pltpu.VMEM((chans, rows, wide), bf16),
            pltpu.VMEM((chans, rows, high), bf16),
            pltpu.VMEM((2, 2 * BLOCK, BLOCK), bf16),
            pltpu.VMEM((chans, rows, cols), bf16),
            dma((chans * cols // BLOCK,)),
        ],
        compiler_params=pltpu.CompilerParams(vmem_limit_bytes=32 * 2**20),
    )(padded, col_disp, row_disp)


def solution(mesh):
    return jax.shard_map(
        local,
        mesh=mesh,
        in_specs=(P("ch", "ty", "tx"), P("ch", None, "ty", "tx")),
        out_specs=P("ch", "ty", "tx"),
        check_vma=False,
    )
```

```python
import functools

import jax
import jax.numpy as jnp
from jax import lax
from jax.experimental import pallas as pl
from jax.experimental.pallas import tpu as pltpu
from jax.sharding import PartitionSpec as P

PATCH = 64
SPAN_Y = 256
SPAN_X = 512
MAX_Y = 12
MAX_X = 60
HY = 16
HX = 64
EPS = 1e-05
LANES = 128
MESH = pl.DeviceIdType.MESH


def bspline(offset):
    mag = jnp.abs(offset)
    near_part = 2.0 / 3.0 - mag * mag + 0.5 * mag * mag * mag
    far_part = (2.0 - mag) * (2.0 - mag) * (2.0 - mag) / 6.0
    return jnp.where(mag < 1.0, near_part, jnp.where(mag < 2.0, far_part, 0.0))


def cubic_kernel(offset):
    a = jnp.maximum(2.0 - jnp.abs(offset), 0.0)
    c = a - 1.0
    b = jnp.maximum(c, 0.0)
    return a * a * (0.5 * c) + b * b * (1.0 - 2.0 * b)


def penalty_band(count):
    band = [[0.0] * count for _ in range(4)]
    coef = (1.0, -2.0, 1.0)
    for q in range(count - 2):
        for a in range(3):
            for b in range(a, 3):
                band[b - a][q + a] += coef[a] * coef[b]
    return band


def iota(dim, shape=(8, LANES)):
    return lax.broadcasted_iota(jnp.int32, shape, dim)


def repeat_for(start, stop, body):
    if stop - start <= 16:
        for i in range(start, stop):
            body(i)
    else:
        lax.fori_loop(start, stop, lambda i, _: (body(i), 0)[1], 0)


def fit_kernel(n_ty, n_tx, lam_y, lam_x, img_v, shift_ref, pad_ref, col_ref, row_ref,
               side_v, sums_v, shift_v, e0_v, msg_v, slots_v, coef_v, pack_v, zero_v,
               own_sem, zero_sem, e0_send, e0_recv, msg_send, msg_recv,
               halo_send, halo_recv):
    chans, rows, cols = img_v.shape
    prow, pcol = rows // PATCH, cols // PATCH
    n = n_ty * n_tx
    ch, ty, tx = lax.axis_index("ch"), lax.axis_index("ty"), lax.axis_index("tx")
    me = ty * n_tx + tx

    def peer_id(p):
        peer = lax.rem(me + p, n)
        return peer, {"ty": peer // n_tx, "tx": lax.rem(peer, n_tx)}

    barrier = pltpu.get_barrier_semaphore()
    partner = {"ch": 1 - ch}
    pl.semaphore_signal(barrier, inc=1, device_id=partner, device_id_type=MESH)

    def greet(p):
        _, where = peer_id(p)
        pl.semaphore_signal(barrier, inc=1, device_id=where, device_id_type=MESH)

    repeat_for(1, n, greet)
    zero_v[...] = jnp.zeros_like(zero_v)

    owns = [
        pltpu.make_async_copy(
            img_v.at[c], pad_ref.at[c, pl.ds(HY, rows), pl.ds(2 * HX, cols)], own_sem.at[c]
        )
        for c in range(chans)
    ]
    for own in owns:
        own.start()
    tail, head = cols - 2 * HX, 2 * HX
    pack_v[0] = jnp.concatenate([img_v[0, :, tail + HX :], img_v[1, :, tail + HX :]], axis=1)
    pack_v[1] = jnp.concatenate([img_v[0, :, :HX], img_v[1, :, :HX]], axis=1)
    span_y = {1: (rows - HY, 0, HY), -1: (0, HY + rows, HY), 0: (0, HY, rows)}
    sides = [(0, 1), (0, -1), (1, 0), (-1, 0), (1, 1), (1, -1), (-1, 1), (-1, -1)]
    halos = []
    for s, (dy, dx) in enumerate(sides):
        sy, qy, ly = span_y[dy]
        if dx == 0:
            src, dst = img_v.at[:, pl.ds(sy, ly)], pad_ref.at[:, pl.ds(qy, ly), pl.ds(2 * HX, cols)]
            zeros = zero_v.at[:, pl.ds(0, ly)]
        else:
            side = 0 if dx == 1 else 1
            src, dst = pack_v.at[side, pl.ds(sy, ly)], side_v.at[side, pl.ds(qy, ly)]
            zeros = zero_v.at[0, pl.ds(0, ly), pl.ds(0, head)]
        to_y, to_x = ty + dy, tx + dx
        from_y, from_x = ty - dy, tx - dx
        has_to = (to_y >= 0) & (to_y < n_ty) & (to_x >= 0) & (to_x < n_tx)
        has_from = (from_y >= 0) & (from_y < n_ty) & (from_x >= 0) & (from_x < n_tx)
        halo = pltpu.make_async_remote_copy(
            src_ref=src, dst_ref=dst, send_sem=halo_send.at[s], recv_sem=halo_recv.at[s],
            device_id={"ty": to_y, "tx": to_x}, device_id_type=MESH,
        )
        fill = pltpu.make_async_copy(zeros, dst, zero_sem.at[s])
        pl.when(jnp.logical_not(has_from))(fill.start)
        halos.append((halo, has_to, has_from, fill))

    sub, lane = iota(0), iota(1)
    per_chan = 2 * prow
    per_dev = chans * per_chan
    ty_block = LANES // per_dev
    blocks = (n_ty + ty_block - 1) // ty_block
    col_sys = sub < chans
    row_sys = (sub >= chans) & (sub < 2 * chans)
    is_rhs = jnp.where(col_sys, (lane // pcol) % 2, (lane // prow) % 2) == 1
    key_y = n_ty * rows // SPAN_Y + 3
    key_x = n_tx * cols // SPAN_X + 3
    per_y, per_x = rows * ty_block // SPAN_Y, cols // SPAN_X
    keys = max(key_y, key_x)
    chunks = max(n_tx, blocks)
    col_pos = (lane % pcol * PATCH).astype(jnp.float32) / SPAN_X + (PATCH / 2.0 / SPAN_X + 1.0)
    row_index = lane // per_dev * prow + lane % prow
    row_pos = (row_index * PATCH).astype(jnp.float32) / SPAN_Y + (PATCH / 2.0 / SPAN_Y + 1.0)
    for q in range(2):
        for c in range(chans):
            part = shift_ref[c, q].astype(jnp.float32)
            for g in range(LANES // pcol):
                shift_v[q, pl.ds(c * prow, prow), pl.ds(g * pcol, pcol)] = part
    ind = (iota(0, (LANES, LANES)) // PATCH == iota(1, (LANES, LANES)) % 2).astype(jnp.float32)

    for c in range(chans):
        for i in range(prow):
            for t in range(cols // LANES):
                part = img_v[c, pl.ds(i * PATCH, PATCH), pl.ds(t * LANES, LANES)].astype(jnp.float32)
                sums_v[pl.ds(t * 8 + c * prow + i, 1), :] = jnp.sum(part * part, axis=0, keepdims=True)
    halves = jnp.dot(sums_v[...], ind, precision=lax.Precision.HIGHEST,
                     preferred_element_type=jnp.float32)
    energy = jnp.zeros((8, LANES), jnp.float32)
    for t in range(cols // LANES):
        energy = jnp.where(lane % pcol // 2 == t, halves[t * 8 : t * 8 + 8], energy)
    energy = energy / (PATCH * PATCH) + EPS

    pl.semaphore_wait(barrier, n)
    e0_copy = pltpu.make_async_remote_copy(
        src_ref=e0_v, dst_ref=e0_v, send_sem=e0_send, recv_sem=e0_recv,
        device_id=partner, device_id_type=MESH,
    )

    @pl.when(ch == 0)
    def _():
        e0_v[...] = energy
        e0_copy.start()

    for halo, has_to, _, _ in halos:
        pl.when(has_to)(halo.start)

    @pl.when(ch == 1)
    def _():
        e0_copy.wait_recv()

    ref_energy = jnp.concatenate([e0_v[0:prow]] * chans, axis=0)
    weight = jnp.sqrt(ref_energy * energy)
    mine = sub // prow == lane // (2 * pcol)
    scaled = jnp.where((lane // pcol) % 2 == 1, weight * shift_v[1], weight)
    msg_v[0:1, :] = jnp.sum(jnp.where(mine, scaled, 0.0), axis=0, keepdims=True)
    first = lane < pcol
    w_rows = jnp.sum(jnp.where(first, weight, 0.0), axis=1, keepdims=True)
    ws_rows = jnp.sum(jnp.where(first, weight * shift_v[0], 0.0), axis=1, keepdims=True)
    base = lax.rem(ty, ty_block) * per_dev + sub // prow * per_chan + sub % prow
    spread = jnp.where(lane == base, w_rows, jnp.where(lane == base + prow, ws_rows, 0.0))
    msg_v[1:2, :] = jnp.sum(spread, axis=0, keepdims=True)
    slots_v[me, 0:2] = msg_v[0:2]

    def msg_copy(p, slot):
        _, where = peer_id(p)
        return pltpu.make_async_remote_copy(
            src_ref=msg_v.at[pl.ds(0, 2)], dst_ref=slots_v.at[slot, pl.ds(0, 2)],
            send_sem=msg_send.at[p], recv_sem=msg_recv.at[slot],
            device_id=where, device_id_type=MESH,
        )

    repeat_for(1, n, lambda p: msg_copy(p, me).start())

    bases = {}
    for t in range(chunks):
        span = set()
        if t < n_tx:
            span |= set(range(t * per_x, t * per_x + per_x + 3))
        if t < blocks:
            span |= set(range(t * per_y, t * per_y + per_y + 3))
        for k in sorted(span):
            if k < keys:
                local = jnp.where(col_sys, col_pos + (t * per_x - k), row_pos + (t * per_y - k))
                bases[k, t] = bspline(local.astype(jnp.float32))

    def msg_wait(p):
        peer, _ = peer_id(p)
        msg_copy(p, peer).wait_recv()

    repeat_for(1, n, msg_wait)

    data_w, data_r = [], []
    for t in range(chunks):
        data = jnp.zeros((8, LANES), jnp.float32)
        if t < n_tx:
            total = slots_v[t, 0:1]
            for y in range(1, n_ty):
                total = total + slots_v[y * n_tx + t, 0:1]
            data = jnp.where(col_sys & (lane // (2 * pcol) == sub), total, data)
        if t < blocks:
            low, high = t * ty_block * n_tx, min(n_ty, (t + 1) * ty_block) * n_tx
            total = slots_v[low, 1:2]
            for y in range(low + 1, high):
                total = total + slots_v[y, 1:2]
            data = jnp.where(row_sys & (lane % per_dev // per_chan == sub - chans), total, data)
        data_w.append(jnp.where(is_rhs, 0.0, data))
        data_r.append(jnp.where(is_rhs, data, 0.0))

    pen_y, pen_x = penalty_band(key_y), penalty_band(key_x)

    def added(d, k):
        rest = 1.0 if d == 0 else 0.0
        at_x = lam_x * pen_x[d][k] if k < key_x else rest
        at_y = lam_y * pen_y[d][k] if k < key_y else rest
        if at_x == at_y == rest:
            return rest
        return jnp.where(col_sys, at_x, jnp.where(row_sys, at_y, rest))

    band, rhs = {}, []
    for k in range(keys):
        for d in range(4):
            if k + d >= keys:
                continue
            total = None
            for t in range(chunks):
                if (k, t) in bases and (k + d, t) in bases:
                    term = bases[k, t] * bases[k + d, t] * data_w[t]
                    total = term if total is None else total + term
            if total is None:
                band[k, d] = jnp.zeros((8, LANES), jnp.float32) + added(d, k)
            else:
                band[k, d] = jnp.broadcast_to(jnp.sum(total, axis=1, keepdims=True), (8, LANES)) + added(d, k)
        total = None
        for t in range(chunks):
            if (k, t) in bases:
                term = bases[k, t] * data_r[t]
                total = term if total is None else total + term
        rhs.append(jnp.broadcast_to(jnp.sum(total, axis=1, keepdims=True), (8, LANES)))

    recips = []
    for k in range(keys):
        recip = 1.0 / band[k, 0]
        recips.append(recip)
        for e in range(1, 4):
            if k + e >= keys:
                break
            factor = band[k, e] * recip
            for f in range(e, 4):
                if k + f < keys:
                    band[k + e, f - e] = band[k + e, f - e] - factor * band[k, f]
            rhs[k + e] = rhs[k + e] - factor * rhs[k]
    solved = [None] * keys
    for k in reversed(range(keys)):
        value = rhs[k]
        for e in range(3, 0, -1):
            if k + e < keys:
                value = value - band[k, e] * solved[k + e]
        solved[k] = value * recips[k]
        coef_v[k] = solved[k]

    lane_f = lane.astype(jnp.float32) + 0.5
    for out_ref, span, size, start, bound in (
        (col_ref, SPAN_X, cols, tx * (cols // SPAN_X), MAX_X),
        (row_ref, SPAN_Y, rows, ty * (rows // SPAN_Y), MAX_Y),
    ):
        tiles = span // LANES
        shape = [
            [bspline((lane_f + u * LANES) / span - e + 1.0) for e in range(4)] for u in range(tiles)
        ]
        for q in range(size // span):
            coefs = [coef_v[start + q + e] for e in range(4)]
            for u in range(tiles):
                total = coefs[0] * shape[u][0]
                for e in range(1, 4):
                    total = total + coefs[e] * shape[u][e]
                at = (q * tiles + u) * LANES
                out_ref[:, at : at + LANES] = bound * jnp.tanh(total / bound)

    for halo, has_to, has_from, fill in halos:
        pl.when(has_from)(halo.wait_recv)
        pl.when(jnp.logical_not(has_from))(fill.wait)
        pl.when(has_to)(halo.wait_send)
    for i in range(2):
        whole = side_v[i]
        other = jnp.concatenate([whole[:, HX:], whole[:, :HX]], axis=1)
        at = 0 if i == 0 else head + cols
        pad_ref[i, :, at : at + head] = other
        pad_ref[1 - i, :, at : at + head] = whole
    for own in owns:
        own.wait()
    pl.when(ch == 0)(e0_copy.wait_send)
    repeat_for(1, n, lambda p: msg_copy(p, me).wait_send())


BLOCK = 256
HALF = 128
PAD = 64


def taps(target, depth, shift):
    low = jnp.floor(target)
    frac = target - low
    weights = [cubic_kernel(float(e) - frac).astype(jnp.bfloat16) for e in (-1, 0, 1, 2)]
    shape = (depth, target.shape[1])
    source = (lax.broadcasted_iota(jnp.int32, shape, 0) - shift).astype(jnp.float32).astype(jnp.bfloat16)
    offset = source - (low - shift).astype(jnp.bfloat16)
    out = jnp.zeros(shape, jnp.bfloat16)
    for e, weight in zip((-1, 0, 1, 2), weights):
        out = jnp.where(offset == e, jnp.broadcast_to(weight, shape), out)
    return out


def warp_kernel(pad_ref, col_ref, row_ref, out_hbm, rows_v, rtaps_v, ctaps_v, out_v, out_sem):
    chans, rows, cols = out_v.shape
    depth = pad_ref.shape[1]
    steps = cols // BLOCK
    lane_f = lax.broadcasted_iota(jnp.int32, (1, HALF), 1).astype(jnp.float32)
    row_f = lax.broadcasted_iota(jnp.int32, (1, rows), 1).astype(jnp.float32)
    for slot in range(2):
        ctaps_v[slot] = jnp.zeros(ctaps_v.shape[1:], jnp.bfloat16)
    for c in range(chans):
        target = row_f + HY + row_ref[chans + c : chans + c + 1, :]
        source = lax.broadcasted_iota(jnp.int32, (depth, rows), 0).astype(jnp.float32)
        rtaps_v[c] = cubic_kernel(source - target).T.astype(jnp.bfloat16)
    copies = []
    for c in range(chans):
        def row_tile(b):
            rows_v[c, :, b * BLOCK : (b + 1) * BLOCK] = jnp.dot(
                rtaps_v[c], pad_ref[c, :, b * BLOCK : (b + 1) * BLOCK],
                preferred_element_type=jnp.float32,
            ).astype(jnp.bfloat16)

        row_tile(0)
        for b in range(steps):
            row_tile(b + 1)
            slot = b % 2
            for h in range(BLOCK // HALF):
                at = b * BLOCK + h * HALF
                target = lane_f + float(PAD) + col_ref[c : c + 1, at : at + HALF]
                ctaps_v[slot, PAD + h * HALF : PAD + (h + 2) * HALF, h * HALF : (h + 1) * HALF] = (
                    taps(target, 2 * HALF, HALF)
                )
            out_v[c, :, b * BLOCK : (b + 1) * BLOCK] = jnp.dot(
                rows_v[c, :, b * BLOCK : (b + 2) * BLOCK], ctaps_v[slot],
                preferred_element_type=jnp.float32,
            ).astype(jnp.bfloat16)
            part = (c, slice(None), pl.ds(b * BLOCK, BLOCK))
            copy = pltpu.make_async_copy(out_v.at[part], out_hbm.at[part], out_sem.at[c * steps + b])
            copy.start()
            copies.append(copy)
    for copy in copies:
        copy.wait()


def local(image_plane, patch_shift):
    n_ty, n_tx = lax.axis_size("ty"), lax.axis_size("tx")
    chans, rows, cols = image_plane.shape
    n = n_ty * n_tx
    lam_y = SPAN_Y / PATCH * (cols * n_tx / PATCH) * (2.0 * rows / SPAN_Y) ** 4
    lam_x = SPAN_X / PATCH * (rows * n_ty / PATCH) * (1.0 * cols / SPAN_X) ** 4
    keys = max(n_ty * rows // SPAN_Y, n_tx * cols // SPAN_X) + 3
    high, wide = rows + 2 * HY, cols + 4 * HX
    f32 = jnp.float32
    dma = pltpu.SemaphoreType.DMA
    vmem = pl.BlockSpec(memory_space=pltpu.VMEM)
    hbm = pl.BlockSpec(memory_space=pltpu.HBM)
    padded, col_disp, row_disp = pl.pallas_call(
        functools.partial(fit_kernel, n_ty, n_tx, lam_y, lam_x),
        out_shape=(
            jax.ShapeDtypeStruct((chans, high, wide), jnp.bfloat16),
            jax.ShapeDtypeStruct((8, cols), f32),
            jax.ShapeDtypeStruct((8, rows), f32),
        ),
        in_specs=[vmem, vmem],
        out_specs=(vmem, vmem, vmem),
        scratch_shapes=[
            pltpu.VMEM((2, high, 2 * HX), jnp.bfloat16),
            pltpu.VMEM((LANES, LANES), f32),
            pltpu.VMEM((2, 8, LANES), f32),
            pltpu.VMEM((8, LANES), f32),
            pltpu.VMEM((8, LANES), f32),
            pltpu.VMEM((n, 8, LANES), f32),
            pltpu.VMEM((keys, 8, LANES), f32),
            pltpu.VMEM((2, rows, 2 * HX), jnp.bfloat16),
            pltpu.VMEM((chans, rows, cols), jnp.bfloat16),
            dma((chans,)), dma((8,)), dma, dma,
            dma((n,)), dma((n,)), dma((8,)), dma((8,)),
        ],
        compiler_params=pltpu.CompilerParams(
            collective_id=0, has_side_effects=True, vmem_limit_bytes=32 * 2**20
        ),
    )(image_plane, patch_shift)
    bf16 = jnp.bfloat16
    return pl.pallas_call(
        warp_kernel,
        out_shape=jax.ShapeDtypeStruct((chans, rows, cols), bf16),
        in_specs=[vmem, vmem, vmem],
        out_specs=hbm,
        scratch_shapes=[
            pltpu.VMEM((chans, rows, wide), bf16),
            pltpu.VMEM((chans, rows, high), bf16),
            pltpu.VMEM((2, 2 * BLOCK, BLOCK), bf16),
            pltpu.VMEM((chans, rows, cols), bf16),
            dma((chans * cols // BLOCK,)),
        ],
        compiler_params=pltpu.CompilerParams(vmem_limit_bytes=32 * 2**20),
    )(padded, col_disp, row_disp)


def solution(mesh):
    return jax.shard_map(
        local,
        mesh=mesh,
        in_specs=(P("ch", "ty", "tx"), P("ch", None, "ty", "tx")),
        out_specs=P("ch", "ty", "tx"),
        check_vma=False,
    )
```

```python
import functools

import jax
import jax.numpy as jnp
from jax import lax
from jax.experimental import pallas as pl
from jax.experimental.pallas import tpu as pltpu
from jax.sharding import PartitionSpec as P

PATCH = 64
SPAN_Y = 256
SPAN_X = 512
MAX_Y = 12
MAX_X = 60
HY = 16
HX = 64
EPS = 1e-05
LANES = 128
MESH = pl.DeviceIdType.MESH


def bspline(offset):
    mag = jnp.abs(offset)
    near_part = 2.0 / 3.0 - mag * mag + 0.5 * mag * mag * mag
    far_part = (2.0 - mag) * (2.0 - mag) * (2.0 - mag) / 6.0
    return jnp.where(mag < 1.0, near_part, jnp.where(mag < 2.0, far_part, 0.0))


def cubic_kernel(offset):
    a = jnp.maximum(2.0 - jnp.abs(offset), 0.0)
    c = a - 1.0
    b = jnp.maximum(c, 0.0)
    return a * a * (0.5 * c) + b * b * (1.0 - 2.0 * b)


def penalty_band(count):
    band = [[0.0] * count for _ in range(4)]
    coef = (1.0, -2.0, 1.0)
    for q in range(count - 2):
        for a in range(3):
            for b in range(a, 3):
                band[b - a][q + a] += coef[a] * coef[b]
    return band


def iota(dim, shape=(8, LANES)):
    return lax.broadcasted_iota(jnp.int32, shape, dim)


def repeat_for(start, stop, body):
    if stop - start <= 16:
        for i in range(start, stop):
            body(i)
    else:
        lax.fori_loop(start, stop, lambda i, _: (body(i), 0)[1], 0)


def fit_kernel(n_ty, n_tx, lam_y, lam_x, img_v, shift_ref, pad_ref, col_ref, row_ref,
               side_v, sums_v, shift_v, e0_v, msg_v, slots_v, coef_v, pack_v, zero_v,
               own_sem, zero_sem, e0_send, e0_recv, msg_send, msg_recv,
               halo_send, halo_recv):
    chans, rows, cols = img_v.shape
    prow, pcol = rows // PATCH, cols // PATCH
    n = n_ty * n_tx
    ch, ty, tx = lax.axis_index("ch"), lax.axis_index("ty"), lax.axis_index("tx")
    me = ty * n_tx + tx

    def peer_id(p):
        peer = lax.rem(me + p, n)
        return peer, {"ty": peer // n_tx, "tx": lax.rem(peer, n_tx)}

    barrier = pltpu.get_barrier_semaphore()
    partner = {"ch": 1 - ch}
    pl.semaphore_signal(barrier, inc=1, device_id=partner, device_id_type=MESH)

    def greet(p):
        _, where = peer_id(p)
        pl.semaphore_signal(barrier, inc=1, device_id=where, device_id_type=MESH)

    repeat_for(1, n, greet)
    zero_v[...] = jnp.zeros_like(zero_v)

    owns = [
        pltpu.make_async_copy(
            img_v.at[c], pad_ref.at[c, pl.ds(HY, rows), pl.ds(2 * HX, cols)], own_sem.at[c]
        )
        for c in range(chans)
    ]
    for own in owns:
        own.start()
    tail, head = cols - 2 * HX, 2 * HX
    pack_v[0] = jnp.concatenate([img_v[0, :, tail + HX :], img_v[1, :, tail + HX :]], axis=1)
    pack_v[1] = jnp.concatenate([img_v[0, :, :HX], img_v[1, :, :HX]], axis=1)
    span_y = {1: (rows - HY, 0, HY), -1: (0, HY + rows, HY), 0: (0, HY, rows)}
    sides = [(0, 1), (0, -1), (1, 0), (-1, 0), (1, 1), (1, -1), (-1, 1), (-1, -1)]
    halos = []
    for s, (dy, dx) in enumerate(sides):
        sy, qy, ly = span_y[dy]
        if dx == 0:
            src, dst = img_v.at[:, pl.ds(sy, ly)], pad_ref.at[:, pl.ds(qy, ly), pl.ds(2 * HX, cols)]
            zeros = zero_v.at[:, pl.ds(0, ly)]
        else:
            side = 0 if dx == 1 else 1
            src, dst = pack_v.at[side, pl.ds(sy, ly)], side_v.at[side, pl.ds(qy, ly)]
            zeros = zero_v.at[0, pl.ds(0, ly), pl.ds(0, head)]
        to_y, to_x = ty + dy, tx + dx
        from_y, from_x = ty - dy, tx - dx
        has_to = (to_y >= 0) & (to_y < n_ty) & (to_x >= 0) & (to_x < n_tx)
        has_from = (from_y >= 0) & (from_y < n_ty) & (from_x >= 0) & (from_x < n_tx)
        halo = pltpu.make_async_remote_copy(
            src_ref=src, dst_ref=dst, send_sem=halo_send.at[s], recv_sem=halo_recv.at[s],
            device_id={"ty": to_y, "tx": to_x}, device_id_type=MESH,
        )
        fill = pltpu.make_async_copy(zeros, dst, zero_sem.at[s])
        pl.when(jnp.logical_not(has_from))(fill.start)
        halos.append((halo, has_to, has_from, fill))

    sub, lane = iota(0), iota(1)
    per_chan = 2 * prow
    per_dev = chans * per_chan
    ty_block = LANES // per_dev
    blocks = (n_ty + ty_block - 1) // ty_block
    col_sys = sub < chans
    row_sys = (sub >= chans) & (sub < 2 * chans)
    is_rhs = jnp.where(col_sys, (lane // pcol) % 2, (lane // prow) % 2) == 1
    key_y = n_ty * rows // SPAN_Y + 3
    key_x = n_tx * cols // SPAN_X + 3
    per_y, per_x = rows * ty_block // SPAN_Y, cols // SPAN_X
    keys = max(key_y, key_x)
    chunks = max(n_tx, blocks)
    col_pos = (lane % pcol * PATCH).astype(jnp.float32) / SPAN_X + (PATCH / 2.0 / SPAN_X + 1.0)
    row_index = lane // per_dev * prow + lane % prow
    row_pos = (row_index * PATCH).astype(jnp.float32) / SPAN_Y + (PATCH / 2.0 / SPAN_Y + 1.0)
    for q in range(2):
        for c in range(chans):
            part = shift_ref[c, q].astype(jnp.float32)
            for g in range(LANES // pcol):
                shift_v[q, pl.ds(c * prow, prow), pl.ds(g * pcol, pcol)] = part
    ind = (iota(0, (LANES, LANES)) // PATCH == iota(1, (LANES, LANES)) % 2).astype(jnp.float32)

    for c in range(chans):
        for i in range(prow):
            for t in range(cols // LANES):
                part = img_v[c, pl.ds(i * PATCH, PATCH), pl.ds(t * LANES, LANES)].astype(jnp.float32)
                sums_v[pl.ds(t * 8 + c * prow + i, 1), :] = jnp.sum(part * part, axis=0, keepdims=True)
    halves = jnp.dot(sums_v[...], ind, precision=lax.Precision.HIGHEST,
                     preferred_element_type=jnp.float32)
    energy = jnp.zeros((8, LANES), jnp.float32)
    for t in range(cols // LANES):
        energy = jnp.where(lane % pcol // 2 == t, halves[t * 8 : t * 8 + 8], energy)
    energy = energy / (PATCH * PATCH) + EPS

    pl.semaphore_wait(barrier, n)
    e0_copy = pltpu.make_async_remote_copy(
        src_ref=e0_v, dst_ref=e0_v, send_sem=e0_send, recv_sem=e0_recv,
        device_id=partner, device_id_type=MESH,
    )

    @pl.when(ch == 0)
    def _():
        e0_v[...] = energy
        e0_copy.start()

    @pl.when(ch == 1)
    def _():
        e0_copy.wait_recv()

    ref_energy = jnp.concatenate([e0_v[0:prow]] * chans, axis=0)
    weight = jnp.sqrt(ref_energy * energy)
    mine = sub // prow == lane // (2 * pcol)
    scaled = jnp.where((lane // pcol) % 2 == 1, weight * shift_v[1], weight)
    msg_v[0:1, :] = jnp.sum(jnp.where(mine, scaled, 0.0), axis=0, keepdims=True)
    first = lane < pcol
    w_rows = jnp.sum(jnp.where(first, weight, 0.0), axis=1, keepdims=True)
    ws_rows = jnp.sum(jnp.where(first, weight * shift_v[0], 0.0), axis=1, keepdims=True)
    base = lax.rem(ty, ty_block) * per_dev + sub // prow * per_chan + sub % prow
    spread = jnp.where(lane == base, w_rows, jnp.where(lane == base + prow, ws_rows, 0.0))
    msg_v[1:2, :] = jnp.sum(spread, axis=0, keepdims=True)
    slots_v[me, 0:2] = msg_v[0:2]

    def msg_copy(p, slot):
        _, where = peer_id(p)
        return pltpu.make_async_remote_copy(
            src_ref=msg_v.at[pl.ds(0, 2)], dst_ref=slots_v.at[slot, pl.ds(0, 2)],
            send_sem=msg_send.at[p], recv_sem=msg_recv.at[slot],
            device_id=where, device_id_type=MESH,
        )

    repeat_for(1, n, lambda p: msg_copy(p, me).start())
    for halo, has_to, _, _ in halos:
        pl.when(has_to)(halo.start)

    bases = {}
    for t in range(chunks):
        span = set()
        if t < n_tx:
            span |= set(range(t * per_x, t * per_x + per_x + 3))
        if t < blocks:
            span |= set(range(t * per_y, t * per_y + per_y + 3))
        for k in sorted(span):
            if k < keys:
                local = jnp.where(col_sys, col_pos + (t * per_x - k), row_pos + (t * per_y - k))
                bases[k, t] = bspline(local.astype(jnp.float32))

    def msg_wait(p):
        peer, _ = peer_id(p)
        msg_copy(p, peer).wait_recv()

    repeat_for(1, n, msg_wait)

    data_w, data_r = [], []
    for t in range(chunks):
        data = jnp.zeros((8, LANES), jnp.float32)
        if t < n_tx:
            total = slots_v[t, 0:1]
            for y in range(1, n_ty):
                total = total + slots_v[y * n_tx + t, 0:1]
            data = jnp.where(col_sys & (lane // (2 * pcol) == sub), total, data)
        if t < blocks:
            low, high = t * ty_block * n_tx, min(n_ty, (t + 1) * ty_block) * n_tx
            total = slots_v[low, 1:2]
            for y in range(low + 1, high):
                total = total + slots_v[y, 1:2]
            data = jnp.where(row_sys & (lane % per_dev // per_chan == sub - chans), total, data)
        data_w.append(jnp.where(is_rhs, 0.0, data))
        data_r.append(jnp.where(is_rhs, data, 0.0))

    pen_y, pen_x = penalty_band(key_y), penalty_band(key_x)

    def added(d, k):
        rest = 1.0 if d == 0 else 0.0
        at_x = lam_x * pen_x[d][k] if k < key_x else rest
        at_y = lam_y * pen_y[d][k] if k < key_y else rest
        if at_x == at_y == rest:
            return rest
        return jnp.where(col_sys, at_x, jnp.where(row_sys, at_y, rest))

    band, rhs = {}, []
    for k in range(keys):
        for d in range(4):
            if k + d >= keys:
                continue
            total = None
            for t in range(chunks):
                if (k, t) in bases and (k + d, t) in bases:
                    term = bases[k, t] * bases[k + d, t] * data_w[t]
                    total = term if total is None else total + term
            if total is None:
                band[k, d] = jnp.zeros((8, LANES), jnp.float32) + added(d, k)
            else:
                band[k, d] = jnp.broadcast_to(jnp.sum(total, axis=1, keepdims=True), (8, LANES)) + added(d, k)
        total = None
        for t in range(chunks):
            if (k, t) in bases:
                term = bases[k, t] * data_r[t]
                total = term if total is None else total + term
        rhs.append(jnp.broadcast_to(jnp.sum(total, axis=1, keepdims=True), (8, LANES)))

    recips = []
    for k in range(keys):
        recip = 1.0 / band[k, 0]
        recips.append(recip)
        for e in range(1, 4):
            if k + e >= keys:
                break
            factor = band[k, e] * recip
            for f in range(e, 4):
                if k + f < keys:
                    band[k + e, f - e] = band[k + e, f - e] - factor * band[k, f]
            rhs[k + e] = rhs[k + e] - factor * rhs[k]
    solved = [None] * keys
    for k in reversed(range(keys)):
        value = rhs[k]
        for e in range(3, 0, -1):
            if k + e < keys:
                value = value - band[k, e] * solved[k + e]
        solved[k] = value * recips[k]
        coef_v[k] = solved[k]

    lane_f = lane.astype(jnp.float32) + 0.5
    for out_ref, span, size, start, bound in (
        (col_ref, SPAN_X, cols, tx * (cols // SPAN_X), MAX_X),
        (row_ref, SPAN_Y, rows, ty * (rows // SPAN_Y), MAX_Y),
    ):
        tiles = span // LANES
        shape = [
            [bspline((lane_f + u * LANES) / span - e + 1.0) for e in range(4)] for u in range(tiles)
        ]
        for q in range(size // span):
            coefs = [coef_v[start + q + e] for e in range(4)]
            for u in range(tiles):
                total = coefs[0] * shape[u][0]
                for e in range(1, 4):
                    total = total + coefs[e] * shape[u][e]
                at = (q * tiles + u) * LANES
                out_ref[:, at : at + LANES] = bound * jnp.tanh(total / bound)

    for halo, has_to, has_from, fill in halos:
        pl.when(has_from)(halo.wait_recv)
        pl.when(jnp.logical_not(has_from))(fill.wait)
        pl.when(has_to)(halo.wait_send)
    for i in range(2):
        whole = side_v[i]
        other = jnp.concatenate([whole[:, HX:], whole[:, :HX]], axis=1)
        at = 0 if i == 0 else head + cols
        pad_ref[i, :, at : at + head] = other
        pad_ref[1 - i, :, at : at + head] = whole
    for own in owns:
        own.wait()
    pl.when(ch == 0)(e0_copy.wait_send)
    repeat_for(1, n, lambda p: msg_copy(p, me).wait_send())


BLOCK = 256
HALF = 128
PAD = 64


def taps(target, depth, shift):
    low = jnp.floor(target)
    frac = target - low
    weights = [cubic_kernel(float(e) - frac).astype(jnp.bfloat16) for e in (-1, 0, 1, 2)]
    shape = (depth, target.shape[1])
    source = (lax.broadcasted_iota(jnp.int32, shape, 0) - shift).astype(jnp.float32).astype(jnp.bfloat16)
    offset = source - (low - shift).astype(jnp.bfloat16)
    out = jnp.zeros(shape, jnp.bfloat16)
    for e, weight in zip((-1, 0, 1, 2), weights):
        out = jnp.where(offset == e, jnp.broadcast_to(weight, shape), out)
    return out


def warp_kernel(pad_ref, col_ref, row_ref, out_hbm, rows_v, rtaps_v, ctaps_v, out_v, out_sem):
    chans, rows, cols = out_v.shape
    depth = pad_ref.shape[1]
    steps = cols // BLOCK
    lane_f = lax.broadcasted_iota(jnp.int32, (1, HALF), 1).astype(jnp.float32)
    row_f = lax.broadcasted_iota(jnp.int32, (1, rows), 1).astype(jnp.float32)
    for slot in range(2):
        ctaps_v[slot] = jnp.zeros(ctaps_v.shape[1:], jnp.bfloat16)
    for c in range(chans):
        target = row_f + HY + row_ref[chans + c : chans + c + 1, :]
        source = lax.broadcasted_iota(jnp.int32, (depth, rows), 0).astype(jnp.float32)
        rtaps_v[c] = cubic_kernel(source - target).T.astype(jnp.bfloat16)
    copies = []
    for c in range(chans):
        def row_tile(b):
            rows_v[c, :, b * BLOCK : (b + 1) * BLOCK] = jnp.dot(
                rtaps_v[c], pad_ref[c, :, b * BLOCK : (b + 1) * BLOCK],
                preferred_element_type=jnp.float32,
            ).astype(jnp.bfloat16)

        row_tile(0)
        for b in range(steps):
            row_tile(b + 1)
            slot = b % 2
            for h in range(BLOCK // HALF):
                at = b * BLOCK + h * HALF
                target = lane_f + float(PAD) + col_ref[c : c + 1, at : at + HALF]
                ctaps_v[slot, PAD + h * HALF : PAD + (h + 2) * HALF, h * HALF : (h + 1) * HALF] = (
                    taps(target, 2 * HALF, HALF)
                )
            out_v[c, :, b * BLOCK : (b + 1) * BLOCK] = jnp.dot(
                rows_v[c, :, b * BLOCK : (b + 2) * BLOCK], ctaps_v[slot],
                preferred_element_type=jnp.float32,
            ).astype(jnp.bfloat16)
            part = (c, slice(None), pl.ds(b * BLOCK, BLOCK))
            copy = pltpu.make_async_copy(out_v.at[part], out_hbm.at[part], out_sem.at[c * steps + b])
            copy.start()
            copies.append(copy)
    for copy in copies:
        copy.wait()


def local(image_plane, patch_shift):
    n_ty, n_tx = lax.axis_size("ty"), lax.axis_size("tx")
    chans, rows, cols = image_plane.shape
    n = n_ty * n_tx
    lam_y = SPAN_Y / PATCH * (cols * n_tx / PATCH) * (2.0 * rows / SPAN_Y) ** 4
    lam_x = SPAN_X / PATCH * (rows * n_ty / PATCH) * (1.0 * cols / SPAN_X) ** 4
    keys = max(n_ty * rows // SPAN_Y, n_tx * cols // SPAN_X) + 3
    high, wide = rows + 2 * HY, cols + 4 * HX
    f32 = jnp.float32
    dma = pltpu.SemaphoreType.DMA
    vmem = pl.BlockSpec(memory_space=pltpu.VMEM)
    hbm = pl.BlockSpec(memory_space=pltpu.HBM)
    padded, col_disp, row_disp = pl.pallas_call(
        functools.partial(fit_kernel, n_ty, n_tx, lam_y, lam_x),
        out_shape=(
            jax.ShapeDtypeStruct((chans, high, wide), jnp.bfloat16),
            jax.ShapeDtypeStruct((8, cols), f32),
            jax.ShapeDtypeStruct((8, rows), f32),
        ),
        in_specs=[vmem, vmem],
        out_specs=(vmem, vmem, vmem),
        scratch_shapes=[
            pltpu.VMEM((2, high, 2 * HX), jnp.bfloat16),
            pltpu.VMEM((LANES, LANES), f32),
            pltpu.VMEM((2, 8, LANES), f32),
            pltpu.VMEM((8, LANES), f32),
            pltpu.VMEM((8, LANES), f32),
            pltpu.VMEM((n, 8, LANES), f32),
            pltpu.VMEM((keys, 8, LANES), f32),
            pltpu.VMEM((2, rows, 2 * HX), jnp.bfloat16),
            pltpu.VMEM((chans, rows, cols), jnp.bfloat16),
            dma((chans,)), dma((8,)), dma, dma,
            dma((n,)), dma((n,)), dma((8,)), dma((8,)),
        ],
        compiler_params=pltpu.CompilerParams(
            collective_id=0, has_side_effects=True, vmem_limit_bytes=32 * 2**20
        ),
    )(image_plane, patch_shift)
    bf16 = jnp.bfloat16
    return pl.pallas_call(
        warp_kernel,
        out_shape=jax.ShapeDtypeStruct((chans, rows, cols), bf16),
        in_specs=[vmem, vmem, vmem],
        out_specs=hbm,
        scratch_shapes=[
            pltpu.VMEM((chans, rows, wide), bf16),
            pltpu.VMEM((chans, rows, high), bf16),
            pltpu.VMEM((2, 2 * BLOCK, BLOCK), bf16),
            pltpu.VMEM((chans, rows, cols), bf16),
            dma((chans * cols // BLOCK,)),
        ],
        compiler_params=pltpu.CompilerParams(vmem_limit_bytes=32 * 2**20),
    )(padded, col_disp, row_disp)


def solution(mesh):
    return jax.shard_map(
        local,
        mesh=mesh,
        in_specs=(P("ch", "ty", "tx"), P("ch", None, "ty", "tx")),
        out_specs=P("ch", "ty", "tx"),
        check_vma=False,
    )
```
